256 devices in a mesh: dp: 16 (over z, x_hi), mp: 16 (over x_lo, y, core).
Axes of the slice: x: 4 (x_hi: 2, x_lo: 2; x = x_hi * 2 + x_lo), y: 4, z: 8, core: 2. Of those that a mesh axis runs over, the one named last changes fastest.
Arguments:
- image_embed: bfloat16 [32768, 1152], P(('dp', 'mp')), may hold values from -0.176776695 to 0.176776695
- text_embed: bfloat16 [32768, 1152], P(('dp', 'mp')), may hold values from -0.176776695 to 0.176776695
- log_scale: float32 [1], replicated, may hold values from 1.1 to 2.3
- logit_bias: float32 [1], replicated, may hold values from -3 to -1
Outputs:
- loss: float32 [1], replicated
- image_grad: float32 [32768, 1152], P(('dp', 'mp'))
- text_grad: float32 [32768, 1152], P(('dp', 'mp'))
The draws below stay inside these ranges and needn't reach their ends.
All inputs are finite; a program needn't handle non-finite values.
Results may differ from the reference program's by a relative error of at most 0.0015.
Values may be sent and summed in bfloat16 or wider, within the bound.
No kernel may reach another device: no remote copies, remote signals or barrier semaphores. Data moves between devices by JAX's collectives and lax.ppermute only.
A program may use at most 128 MiB of HBM per device.

```python
import jax
import jax.numpy as jnp
from jax import lax

D = 1152
STEPS = 2
GROUP = 2048
BATCH = 32768
N_DP = 16


def shared_direction(key):
    direction = jax.random.normal(key, (D,), jnp.float32)
    return direction / jnp.sqrt(jnp.sum(direction * direction))


def build_rows(key, base, power, start, reach):
    position = jnp.arange(BATCH, dtype=jnp.float32) / BATCH
    weight = start + reach * position ** power
    noise = jax.random.normal(key, (BATCH, D), jnp.float32)
    noise = noise * D ** (-0.5)
    rows = weight[:, None] * base[None, :] + jnp.sqrt(1.0 - weight * weight)[:, None] * noise
    limit = 6.0 * D ** (-0.5)
    return jnp.clip(rows, -limit, limit).astype(jnp.bfloat16)


def draw_image_embed(key, part):
    base = shared_direction(key)
    key = jax.random.fold_in(key, 11)
    return build_rows(key, base, 1.0, 0.1, 0.85)


def draw_text_embed(key, part):
    base = shared_direction(key)
    key = jax.random.fold_in(key, 23)
    return build_rows(key, base, 1.0, 0.1, 0.85)


def setup_inputs(seed: int = 0) -> dict:
    keys = jax.random.split(jax.random.key(seed), 5)
    return {
        "image_embed": draw_image_embed(jax.random.fold_in(keys[4], 71), 0),
        "text_embed": draw_text_embed(jax.random.fold_in(keys[4], 71), 0),
        "log_scale": jnp.clip(jax.random.uniform(keys[2], (1,), jnp.float32, 1.1, 2.3), 1.1, 2.3),
        "logit_bias": jnp.clip(jax.random.uniform(keys[3], (1,), jnp.float32, -3.0, -1.0), -3.0, -1.0),
    }


def unit_rows(raw):
    values = raw.astype(jnp.float32)
    norm = jnp.sqrt(lax.optimization_barrier(jnp.sum(values * values, axis=1, keepdims=True)) + 1e-06)
    unit = values / norm
    return (unit, unit.astype(jnp.bfloat16), norm)

def back_norm(hat, unit, norm):
    return (hat - unit * lax.optimization_barrier(jnp.sum(unit * hat, axis=1, keepdims=True))) / norm

def reference(image_embed, text_embed, log_scale, logit_bias):
    image_unit, image_low, image_norm = unit_rows(image_embed)
    text_unit, text_low, text_norm = unit_rows(text_embed)
    scale = jnp.exp(log_scale[0])
    bias = logit_bias[0]
    image_hat = jnp.zeros((BATCH, D), jnp.float32)
    text_hat = jnp.zeros((BATCH, D), jnp.float32)
    total = jnp.zeros((), jnp.float32)
    for group in range(N_DP):
        image_part = image_low[group * GROUP:(group + 1) * GROUP]
        for step in range(STEPS):
            other = (group - step) % N_DP
            text_part = text_low[other * GROUP:(other + 1) * GROUP]
            logits = scale * jnp.dot(image_part, text_part.T, preferred_element_type=jnp.float32) + bias
            if step == 0:
                label = 2.0 * jnp.eye(GROUP, dtype=jnp.float32) - 1.0
            else:
                label = -jnp.ones((GROUP, GROUP), jnp.float32)
            total = total + jnp.sum(jax.nn.softplus(-label * logits))
            coef = (-label * jax.nn.sigmoid(-label * logits)).astype(jnp.bfloat16)
            image_hat = image_hat.at[group * GROUP:(group + 1) * GROUP].add(jnp.dot(coef, text_part, preferred_element_type=jnp.float32))
            text_hat = text_hat.at[other * GROUP:(other + 1) * GROUP].add(jnp.dot(coef.T, image_part, preferred_element_type=jnp.float32))
    loss = jnp.reshape(total / (BATCH * STEPS * GROUP), (1,))
    image_grad = back_norm(scale * image_hat, image_unit, image_norm)
    text_grad = back_norm(scale * text_hat, text_unit, text_norm)
    return (loss, image_grad, text_grad)
```

```python
import jax
import jax.numpy as jnp
from jax import lax
from jax.experimental import pallas as pl
from jax.experimental.pallas import tpu as pltpu
from jax.sharding import Mesh, PartitionSpec as P

STEPS = 2
ROWS = 128
TILE = 256
AXES = ("z", "xh", "xl", "y", "c")
SHAPE = (8, 2, 2, 4, 2)
VMEM_LIMIT = 48 * 1024 * 1024


def low_rows_kernel(image_ref, text_ref, image_low_ref, text_low_ref):
    for raw_ref, low_ref in ((image_ref, image_low_ref), (text_ref, text_low_ref)):
        values = raw_ref[...].astype(jnp.float32)
        norm = jnp.sqrt(jnp.sum(values * values, axis=1, keepdims=True) + 1e-06)
        low_ref[...] = (values / norm).astype(jnp.bfloat16)


def low_rows(image, text):
    shape = jax.ShapeDtypeStruct(image.shape, jnp.bfloat16)
    return pl.pallas_call(low_rows_kernel, out_shape=(shape, shape), name="low_rows")(image, text)


def pair_kernel(scalar_ref, i0, i1, i2, i3, t0, t1, t2, t3, s0, s1, s2, s3,
                ih0, ih1, ih2, ih3, th0, th1, thx, sh0, sh1, shx, loss_ref,
                images, texts, coefs):
    scale = scalar_ref[0]
    bias = scalar_ref[1]
    for n, ref in enumerate((i0, i1, i2, i3)):
        images[pl.ds(n * ROWS, ROWS), :] = ref[...]
    for n, ref in enumerate((s0, s1, s2, s3, t0, t1, t2, t3)):
        texts[pl.ds(n * ROWS, ROWS), :] = ref[...]
    total = jnp.zeros((8, TILE), jnp.float32)
    for tile in range(8 * ROWS // TILE):
        columns = pl.ds(tile * TILE, TILE)
        z = scale * lax.dot_general(
            images[...], texts[columns, :], (((1,), (1,)), ((), ())),
            preferred_element_type=jnp.float32) + bias
        if tile == 4 * ROWS // TILE:
            row = lax.broadcasted_iota(jnp.int32, z.shape, 0)
            column = lax.broadcasted_iota(jnp.int32, z.shape, 1)
            positive = row == column
            positive = positive & (row < ROWS)
            z = jnp.where(positive, -z, z)
        small = jnp.exp(-jnp.abs(z))
        term = jnp.maximum(z, 0.0) + jnp.log1p(small)
        coef = jnp.where(z >= 0.0, 1.0, small) / (1.0 + small)
        if tile == 4 * ROWS // TILE:
            coef = jnp.where(positive, -coef, coef)
        total = total + jnp.sum(term.reshape(-1, 8, TILE), axis=0)
        low = coef.astype(jnp.bfloat16)
        coefs[:, columns] = low
        update = lax.dot_general(
            low, images[...], (((0,), (0,)), ((), ())), preferred_element_type=jnp.float32)
        if tile == 0:
            sh0[...] = update[:ROWS]
            sh1[...] = update[ROWS:]
        elif tile == 1:
            shx[...] = update
        elif tile == 2:
            th0[...] = update[:ROWS]
            th1[...] = update[ROWS:]
        else:
            thx[...] = update
    hat = jnp.dot(coefs[...], texts[...], preferred_element_type=jnp.float32)
    for n, ref in enumerate((ih0, ih1, ih2, ih3)):
        ref[...] = hat[n * ROWS:(n + 1) * ROWS]
    loss_ref[...] = jnp.sum(total.reshape(8, TILE // 128, 128), axis=1)


def pairs(scalars, images, texts, shifted):
    width = images[0].shape[1]
    block = jax.ShapeDtypeStruct((ROWS, width), jnp.float32)
    double = jax.ShapeDtypeStruct((2 * ROWS, width), jnp.float32)
    vmem = pl.BlockSpec(memory_space=pltpu.VMEM)
    return pl.pallas_call(
        pair_kernel,
        out_shape=(block,) * 4 + (block, block, double) * 2 + (jax.ShapeDtypeStruct((8, 128), jnp.float32),),
        in_specs=[pl.BlockSpec(memory_space=pltpu.SMEM)] + [vmem] * 12,
        out_specs=(vmem,) * 11,
        scratch_shapes=[
            pltpu.VMEM((4 * ROWS, width), jnp.bfloat16),
            pltpu.VMEM((8 * ROWS, width), jnp.bfloat16),
            pltpu.VMEM((4 * ROWS, 8 * ROWS), jnp.bfloat16),
        ],
        compiler_params=pltpu.CompilerParams(vmem_limit_bytes=VMEM_LIMIT),
        name="pairs",
    )(scalars, *images, *texts, *shifted)


def flip(block, axis, bit=1):
    size = SHAPE[AXES.index(axis)]
    return lax.ppermute(block, axis, [(i, i ^ bit) for i in range(size)])


def turn(block, distance):
    return lax.ppermute(block, "y", [(i, (i + distance) % 4) for i in range(4)])


def next_group():
    route = []
    for group in range(16):
        for side in range(2):
            route.append((group * 2 + side, ((group + 1) % 16) * 2 + 1 - side))
    return route


def forward(block):
    return lax.ppermute(block, ("z", "xh", "xl"), next_group())


def backward(block):
    return lax.ppermute(block, ("z", "xh", "xl"), [(j, i) for i, j in next_group()])


def narrow(block):
    return (block * 32.0).astype(jnp.float16)


def widen(block):
    return block.astype(jnp.float32) * (1.0 / 32.0)


def back_norm(hat, raw):
    values = raw.astype(jnp.float32)
    norm = jnp.sqrt(jnp.sum(values * values, axis=1, keepdims=True) + 1e-06)
    unit = values / norm
    return (hat - unit * jnp.sum(unit * hat, axis=1, keepdims=True)) / norm


def body(image_embed, text_embed, log_scale, logit_bias):
    scale = jnp.exp(log_scale[0])
    scalars = jnp.stack([scale, logit_bias[0]])
    image_low, text_low = low_rows(image_embed, text_embed)
    s0 = forward(text_low)
    t1 = flip(text_low, "xl")
    images = [image_low] + [turn(image_low, k) for k in (1, 2, 3)]
    t23 = flip(jnp.concatenate([text_low, t1]), "c")
    s1 = flip(s0, "xl")
    s23 = flip(jnp.concatenate([s0, s1]), "c")
    texts = [text_low, t1, t23[:ROWS], t23[ROWS:]]
    shifted = [s0, s1, s23[:ROWS], s23[ROWS:]]
    ih0, ih1, ih2, ih3, th0, th1, thx, sh0, sh1, shx, loss = pairs(scalars, images, texts, shifted)
    own = [turn(narrow(part), -k) for k, part in ((1, ih1), (2, ih2), (3, ih3))]
    sc = flip(shx, "c")
    tc = flip(thx, "c")
    sx = flip(narrow(sh1 + sc[ROWS:]), "xl")
    tx = flip(narrow(th1 + tc[ROWS:]), "xl")
    back = backward(narrow(sh0 + sc[:ROWS] + widen(sx)))
    for axis, bit in (("c", 1), ("xl", 1), ("y", 1), ("y", 2), ("xh", 1), ("z", 1), ("z", 2), ("z", 4)):
        loss = loss + flip(loss, axis, bit)
    count = ROWS * 256 * STEPS * ROWS * 16
    loss = jnp.reshape(jnp.sum(loss) / count, (1,))
    image_hat = ih0 + widen(own[0]) + widen(own[1]) + widen(own[2])
    text_hat = th0 + tc[:ROWS] + widen(tx) + widen(back)
    return loss, back_norm(scale * image_hat, image_embed), back_norm(scale * text_hat, text_embed)


def solution(mesh):
    grid = Mesh(mesh.devices.reshape(SHAPE), AXES)
    rows = P(AXES, None)
    return jax.shard_map(
        body, mesh=grid, in_specs=(rows, rows, P(), P()), out_specs=(P(), rows, rows), check_vma=False)
```

```python
import jax
import jax.numpy as jnp
from jax import lax
from jax.experimental import pallas as pl
from jax.experimental.pallas import tpu as pltpu
from jax.sharding import Mesh, PartitionSpec as P

STEPS = 2
ROWS = 128
TILE = 256
AXES = ("z", "xh", "xl", "y", "c")
SHAPE = (8, 2, 2, 4, 2)
VMEM_LIMIT = 28 * 1024 * 1024
VMEM = pl.BlockSpec(memory_space=pltpu.VMEM)
PARAMS = pltpu.CompilerParams(vmem_limit_bytes=VMEM_LIMIT)


def low_rows_kernel(image_ref, text_ref, image_low_ref, text_low_ref):
    for raw_ref, low_ref in ((text_ref, text_low_ref), (image_ref, image_low_ref)):
        values = raw_ref[...].astype(jnp.float32)
        norm = jnp.sqrt(jnp.sum(values * values, axis=1, keepdims=True) + 1e-06)
        low_ref[...] = (values / norm).astype(jnp.bfloat16)


def low_rows(image, text):
    shape = jax.ShapeDtypeStruct(image.shape, jnp.bfloat16)
    return pl.pallas_call(low_rows_kernel, out_shape=(shape, shape), name="low_rows")(image, text)


def score_kernel(scalar_ref, i0, i1, i2, i3, t0, t1, s0, s1, tx, sx, images, texts, coefs, loss_ref):
    scale = scalar_ref[0]
    bias = scalar_ref[1]
    for n, ref in enumerate((i0, i1, i2, i3)):
        images[pl.ds(n * ROWS, ROWS), :] = ref[...]
    for n, ref in enumerate((t0, t1, s0, s1)):
        texts[pl.ds(n * ROWS, ROWS), :] = ref[...]
    texts[pl.ds(4 * ROWS, 3 * ROWS), :] = tx[...]
    texts[pl.ds(7 * ROWS, ROWS), :] = sx[...]
    total = jnp.zeros((8, TILE), jnp.float32)
    for tile in range(8 * ROWS // TILE):
        columns = pl.ds(tile * TILE, TILE)
        z = scale * lax.dot_general(
            images[...], texts[columns, :], (((1,), (1,)), ((), ())),
            preferred_element_type=jnp.float32) + bias
        if tile == 0:
            row = lax.broadcasted_iota(jnp.int32, z.shape, 0)
            column = lax.broadcasted_iota(jnp.int32, z.shape, 1)
            positive = (row == column) & (row < ROWS)
            z = jnp.where(positive, -z, z)
        small = jnp.exp(-jnp.abs(z))
        term = jnp.maximum(z, 0.0) + jnp.log1p(small)
        coef = jnp.where(z >= 0.0, 1.0, small) / (1.0 + small)
        if tile == 0:
            coef = jnp.where(positive, -coef, coef)
        total = total + jnp.sum(term.reshape(-1, 8, TILE), axis=0)
        coefs[:, columns] = coef.astype(jnp.bfloat16)
    loss_ref[...] = total[:, :128] + total[:, 128:]


def score(scalars, *blocks):
    width = blocks[0].shape[1]
    return pl.pallas_call(
        score_kernel,
        out_shape=(
            jax.ShapeDtypeStruct((4 * ROWS, width), jnp.bfloat16),
            jax.ShapeDtypeStruct((8 * ROWS, width), jnp.bfloat16),
            jax.ShapeDtypeStruct((4 * ROWS, 8 * ROWS), jnp.bfloat16),
            jax.ShapeDtypeStruct((8, 128), jnp.float32),
        ),
        in_specs=[pl.BlockSpec(memory_space=pltpu.SMEM)] + [VMEM] * len(blocks),
        out_specs=(VMEM,) * 4,
        compiler_params=PARAMS,
        name="score",
    )(scalars, *blocks)


def text_sums_kernel(coefs, images, t0, t1, s0, s1, others):
    for tile, refs in enumerate(((t0, t1), (s0, s1))):
        update = lax.dot_general(
            coefs[:, tile * TILE:(tile + 1) * TILE], images[...], (((0,), (0,)), ((), ())),
            preferred_element_type=jnp.float32)
        refs[0][...] = update[:ROWS]
        refs[1][...] = update[ROWS:]
    for tile in range(2):
        others[pl.ds(tile * TILE, TILE), :] = lax.dot_general(
            coefs[:, (tile + 2) * TILE:(tile + 3) * TILE], images[...], (((0,), (0,)), ((), ())),
            preferred_element_type=jnp.float32)


def text_sums(coefs, images):
    width = images.shape[1]
    block = jax.ShapeDtypeStruct((ROWS, width), jnp.float32)
    return pl.pallas_call(
        text_sums_kernel,
        out_shape=(block,) * 4 + (jax.ShapeDtypeStruct((4 * ROWS, width), jnp.float32),),
        in_specs=[VMEM] * 2, out_specs=(VMEM,) * 5, compiler_params=PARAMS, name="text_sums",
    )(coefs, images)


def image_sums_kernel(coefs, texts, *outs):
    for half in range(2):
        hat = jnp.dot(coefs[pl.ds(half * TILE, TILE), :], texts[...], preferred_element_type=jnp.float32)
        outs[2 * half][...] = hat[:ROWS]
        outs[2 * half + 1][...] = hat[ROWS:]


def image_sums(coefs, texts):
    block = jax.ShapeDtypeStruct((ROWS, texts.shape[1]), jnp.float32)
    return pl.pallas_call(
        image_sums_kernel, out_shape=(block,) * 4,
        in_specs=[VMEM] * 2, out_specs=(VMEM,) * 4, compiler_params=PARAMS, name="image_sums",
    )(coefs, texts)


def flip(block, axis, bit=1):
    size = SHAPE[AXES.index(axis)]
    return lax.ppermute(block, axis, [(i, i ^ bit) for i in range(size)])


def turn(block, distance):
    return lax.ppermute(block, "y", [(i, (i + distance) % 4) for i in range(4)])


def swap(route):
    return [(j, i) for i, j in route]


def next_group():
    return [
        (group * 2 + side, ((group + 1) % 16) * 2 + 1 - side) for group in range(16) for side in range(2)]


def forward(block):
    return lax.ppermute(block, ("z", "xh", "xl"), next_group())


def backward(block):
    return lax.ppermute(block, ("z", "xh", "xl"), swap(next_group()))


def far_text():
    route = [((a * 4 + y) * 2, (b * 4 + y) * 2) for a, b in next_group() for y in range(4)]
    route += [((a * 4 + y) * 2 + 1, ((a ^ 1) * 4 + y) * 2 + 1) for a in range(32) for y in range(4)]
    return route


def far_image():
    return [(y * 2, (y + 1) % 4 * 2) for y in range(4)] + [(y * 2 + 1, (y + 3) % 4 * 2 + 1) for y in range(4)]


def narrow(block):
    return (block * 32.0).astype(jnp.float16)


def widen(block):
    return block.astype(jnp.float32) * (1.0 / 32.0)


def back_norm(hat, raw):
    values = raw.astype(jnp.float32)
    norm = jnp.sqrt(jnp.sum(values * values, axis=1, keepdims=True) + 1e-06)
    unit = values / norm
    return (hat - unit * jnp.sum(unit * hat, axis=1, keepdims=True)) / norm


def together(*arrays):
    return lax.optimization_barrier(arrays)


def spread(loss, axes, routes):
    return loss + sum(lax.ppermute(loss, axes, route) for route in routes)


def body(image_embed, text_embed, log_scale, logit_bias):
    scale = jnp.exp(log_scale[0])
    scalars = jnp.stack([scale, logit_bias[0]])
    first = lax.axis_index("c") == 0
    i0, t0 = low_rows(image_embed, text_embed)

    s0, t1, ia, ib = together(forward(t0), flip(t0, "xl"), turn(i0, 1), turn(i0, -1))

    s1 = lax.ppermute(jnp.where(first, t1, s0), ("z", "xh", "xl", "y", "c"), far_text())
    i2 = lax.ppermute(jnp.where(first, ia, ib), ("y", "c"), far_image())
    tx = flip(jnp.concatenate([t0, t1, s0]), "c")
    s1, i2, tx = together(s1, i2, tx)
    sx = flip(s1, "c")

    images, texts, coefs, loss = score(scalars, i0, ia, ib, i2, t0, t1, s0, s1, tx, sx)

    ht0, ht1, hs0, hs1, others = text_sums(coefs, images)
    loss = loss + flip(loss, "c")
    others, loss = together(narrow(others), loss)
    other = flip(others, "c")
    hi0, hia, hib, hi2 = image_sums(coefs, texts)
    loss = loss + flip(loss, "xl")
    other, loss, hi2 = together(other, loss, hi2)
    ht0, ht1, hs0, hs1 = [
        own + widen(other[n * ROWS:(n + 1) * ROWS]) for n, own in enumerate((ht0, ht1, hs0, hs1))]

    r2 = lax.ppermute(narrow(hi2), ("y", "c"), swap(far_image()))
    rs = lax.ppermute(narrow(hs1), ("z", "xh", "xl", "y", "c"), swap(far_text()))
    loss = spread(loss, "y", [[(i, (i + k) % 4) for i in range(4)] for k in (1, 2, 3)])
    r2, rs, loss = together(r2, rs, loss)
    r2, rs = widen(r2), widen(rs)
    hia = hia + jnp.where(first, r2, 0.0)
    hib = hib + jnp.where(first, 0.0, r2)
    ht1 = ht1 + jnp.where(first, rs, 0.0)
    hs0 = hs0 + jnp.where(first, 0.0, rs)

    loss = spread(loss, ("z", "xh"), [[(i, i ^ k) for i in range(16)] for k in (1, 2, 3)])
    back = (backward(narrow(hs0)), flip(narrow(ht1), "xl"), turn(narrow(hia), -1), turn(narrow(hib), 1))
    back, loss = together(back, loss)
    text_hat = ht0 + widen(back[0]) + widen(back[1])
    image_hat = hi0 + widen(back[2]) + widen(back[3])
    loss = spread(loss, "z", [[(i, i ^ k) for i in range(8)] for k in (2, 4, 6)])
    count = ROWS * 256 * STEPS * ROWS * 16
    loss = jnp.reshape(jnp.sum(loss) / count, (1,))
    return loss, back_norm(scale * image_hat, image_embed), back_norm(scale * text_hat, text_embed)


def solution(mesh):
    grid = Mesh(mesh.devices.reshape(SHAPE), AXES)
    rows = P(AXES, None)
    return jax.shard_map(
        body, mesh=grid, in_specs=(rows, rows, P(), P()), out_specs=(P(), rows, rows), check_vma=False)
```

```python
import jax
import jax.numpy as jnp
from jax import lax
from jax.experimental import pallas as pl
from jax.experimental.pallas import tpu as pltpu
from jax.sharding import Mesh, PartitionSpec as P

STEPS = 2
ROWS = 128
TILE = 256
AXES = ("z", "xh", "xl", "y", "c")
SHAPE = (8, 2, 2, 4, 2)
VMEM = pl.BlockSpec(memory_space=pltpu.VMEM)
SMEM = pl.BlockSpec(memory_space=pltpu.SMEM)
F32 = jnp.float32
BF16 = jnp.bfloat16


def call(kernel, outs, cost, limit, *args, scratch=()):
    shapes = tuple(jax.ShapeDtypeStruct(shape, dtype) for shape, dtype in outs)
    return pl.pallas_call(
        kernel,
        out_shape=shapes,
        in_specs=[SMEM if a.ndim == 1 else VMEM for a in args],
        out_specs=tuple(SMEM if len(s.shape) == 1 else VMEM for s in shapes),
        scratch_shapes=list(scratch),
        compiler_params=pltpu.CompilerParams(vmem_limit_bytes=limit * 2**20),
        cost_estimate=pl.CostEstimate(flops=int(cost * 1.0e9), bytes_accessed=int(cost * 3.0e6), transcendentals=0),
        name=kernel.__name__,
    )(*args)


def inverse_norm(rows):
    values = rows.astype(F32)
    return 1.0 / jnp.sqrt(jnp.sum(values * values, axis=1, keepdims=True) + 1e-06)


def as_row(column):
    eye = lax.broadcasted_iota(jnp.int32, (ROWS, ROWS), 0) == lax.broadcasted_iota(jnp.int32, (ROWS, ROWS), 1)
    parts = [
        jnp.sum(jnp.where(eye, column[n:n + ROWS], 0.0), axis=0, keepdims=True)
        for n in range(0, column.shape[0], ROWS)]
    return jnp.concatenate(parts, axis=1) if len(parts) > 1 else parts[0]


def dot_t(a, b):
    return lax.dot_general(a, b, (((1,), (1,)), ((), ())), preferred_element_type=F32)


def t_dot(a, b):
    return lax.dot_general(a, b, (((0,), (0,)), ((), ())), preferred_element_type=F32)


def dot(a, b):
    return jnp.dot(a, b, preferred_element_type=F32)


def terms(scalar_ref, products, image_inverse, text_inverse, own=False):
    z = products * (scalar_ref[0] * image_inverse) * text_inverse + scalar_ref[1]
    if own:
        row = lax.broadcasted_iota(jnp.int32, z.shape, 0)
        positive = (row == lax.broadcasted_iota(jnp.int32, z.shape, 1)) & (row < ROWS)
        z = jnp.where(positive, -z, z)
    small = jnp.exp(-jnp.abs(z))
    term = jnp.maximum(z, 0.0) + jnp.log1p(small)
    coef = jnp.where(z >= 0.0, 1.0, small) / (1.0 + small)
    if own:
        coef = jnp.where(positive, -coef, coef)
    total = sum(
        jnp.sum(term[:, n:n + 128].reshape(-1, 8, 128), axis=0) for n in range(0, z.shape[1], 128))
    return total, (coef * text_inverse).astype(BF16), (coef * image_inverse).astype(BF16)


def near(scalar_ref, i0, ia, ib, t0, t1, s0, t0x, t1x, s0x,
         images, texts, image_inverse, text_inverse, loss, ht0, ht1, hs0, htx, hi, coefs):
    for n, ref in enumerate((i0, ia, ib)):
        images[pl.ds(n * ROWS, ROWS), :] = ref[...]
    for n, ref in enumerate((t0, t1, s0, t0x, t1x, s0x)):
        texts[pl.ds(n * ROWS, ROWS), :] = ref[...]
    column = inverse_norm(images[...])
    image_inverse[...] = jnp.broadcast_to(column, image_inverse.shape)
    total = jnp.zeros((8, 128), F32)
    outs = (ht0, ht1, hs0)
    for tile in range(3):
        span = pl.ds(tile * TILE, TILE)
        block = texts[span, :]
        row = as_row(inverse_norm(block))
        text_inverse[:, span] = jnp.broadcast_to(row, (8, TILE))
        part, by_text, by_image = terms(scalar_ref, dot_t(images[...], block), column, row, own=tile == 0)
        total = total + part
        coefs[:, span] = by_text
        update = t_dot(by_image, images[...])
        for half in range(2):
            n = 2 * tile + half
            piece = update[half * ROWS:(half + 1) * ROWS]
            if n < 3:
                outs[n][...] = piece
            else:
                htx[pl.ds((n - 3) * ROWS, ROWS), :] = piece
    hi[...] = dot(coefs[...], texts[...])
    loss[...] = total


def far(scalar_ref, i2, s1, sx, images, texts, image_inverse, text_inverse, loss_in,
        loss, by_near_text, by_near_image, by_far_text, by_far_image, four, pair):
    four[pl.ds(0, 3 * ROWS), :] = images[...]
    four[pl.ds(3 * ROWS, ROWS), :] = i2[...]
    pair[pl.ds(0, ROWS), :] = s1[...]
    pair[pl.ds(ROWS, ROWS), :] = sx[...]
    column = inverse_norm(i2[...])
    total, by_text, by_image = terms(scalar_ref, dot_t(i2[...], texts[...]), column, text_inverse[0:1, :])
    by_near_text[...] = by_text
    by_near_image[...] = by_image
    columns = jnp.concatenate([image_inverse[:, 0:1], column], axis=0)
    part, by_text, by_image = terms(
        scalar_ref, dot_t(four[...], pair[...]), columns, as_row(inverse_norm(pair[...])))
    by_far_text[...] = by_text
    by_far_image[...] = by_image
    loss[...] = loss_in[...] + total + part


def sums(core_ref, by_near_text, by_near_image, by_far_text, by_far_image, i2, four, pair, texts,
         ht0, ht1, hs0, htx, hi, own_text, own_image, blocks):
    second = core_ref[0]

    def put(on_first, on_second, value):
        at = pl.multiple_of((on_first + (on_second - on_first) * second) * ROWS, ROWS)
        blocks[pl.ds(at, ROWS), :] = value

    for n, old in enumerate((ht0, ht1, hs0)):
        value = old[...] + t_dot(by_near_image[:, n * ROWS:(n + 1) * ROWS], i2[...])
        if n == 0:
            own_text[...] = value
        else:
            put(7 + 2 * (n - 1), 1 + 2 * (n - 1) + 1, value)
    for n in range(3):
        value = htx[pl.ds(n * ROWS, ROWS), :] + t_dot(
            by_near_image[:, (n + 3) * ROWS:(n + 4) * ROWS], i2[...])
        if n == 0:
            blocks[pl.ds(0, ROWS), :] = value
        else:
            put(7 + 2 * (n - 1) + 1, 1 + 2 * (n - 1), value)
    value = t_dot(by_far_image[...], four[...])
    put(11, 6, value[:ROWS])
    put(12, 5, value[ROWS:])
    for n in range(3):
        put(2 + 2 * n, 7 + 2 * n, jnp.zeros_like(own_text))
    rest = dot(by_far_text[...], pair[...])
    own_image[...] = hi[pl.ds(0, ROWS), :] + rest[:ROWS]
    for n in (1, 2):
        put(2 * n - 1, 6 + 2 * n, hi[pl.ds(n * ROWS, ROWS), :] + rest[n * ROWS:(n + 1) * ROWS])
    put(5, 12, dot(by_near_text[...], texts[...]) + rest[3 * ROWS:])


def everyone(loss, out):
    out[...] = jnp.broadcast_to(jnp.sum(loss[...], axis=0, keepdims=True), out.shape)


def finish(scalar_ref, raw, hat_ref, *rest):
    if len(rest) == 3:
        parts, out, loss = rest
        loss[0] = jnp.sum(parts[...]) / (ROWS * 256 * STEPS * ROWS * 16)
    else:
        out, = rest
    inverse = inverse_norm(raw[...])
    unit = raw[...].astype(F32) * inverse
    hat = scalar_ref[0] * hat_ref[...]
    out[...] = (hat - unit * jnp.sum(unit * hat, axis=1, keepdims=True)) * inverse


def inner(group, side, y):
    return group, 1 - side, y


def outer(group, side, y):
    return (group + 1) % 16, 1 - side, y


def outer_back(group, side, y):
    return (group + 15) % 16, 1 - side, y


def far_back(group, side, y):
    return (group + 15) % 16, side, y


def up(group, side, y):
    return group, side, (y + 1) % 4


def down(group, side, y):
    return group, side, (y + 3) % 4


def across(group, side, y):
    return group, side, (y + 2) % 4


def move(block, first, second=None):
    route = []
    for chip in range(128):
        place = (chip // 8, chip // 4 % 2, chip % 4)
        for core, to in enumerate((first, second or first)):
            group, side, y = to(*place)
            route.append((chip * 2 + core, (group * 8 + side * 4 + y) * 2 + core))
    return lax.ppermute(block, AXES, route)


def swap_cores(block):
    return lax.ppermute(block, "c", [(0, 1), (1, 0)])


def narrow(block):
    return (block * 32.0).astype(jnp.float16)


def widen(block):
    return block.astype(F32) * (1.0 / 32.0)


def together(*arrays):
    return lax.optimization_barrier(arrays)


def body(image_embed, text_embed, log_scale, logit_bias):
    width = image_embed.shape[1]
    scalars = jnp.stack([jnp.exp(log_scale[0]), logit_bias[0]])
    core = jnp.reshape(lax.axis_index("c"), (1,))
    first = lax.axis_index("c") == 0
    i0, t0 = image_embed, text_embed
    block = ((ROWS, width), F32)

    t0x, ib, ia, t1, s0 = together(swap_cores(t0), move(i0, down), move(i0, up), move(t0, inner), move(t0, outer))

    s1 = move(jnp.where(first, t1, s0), outer, inner)
    i2 = move(jnp.where(first, ia, ib), up, down)
    t1x, s0x = swap_cores(t1), swap_cores(s0)
    images, texts, image_inverse, text_inverse, loss, ht0, ht1, hs0, htx, hi = call(
        near,
        (((3 * ROWS, width), BF16), ((6 * ROWS, width), BF16), ((3 * ROWS, 128), F32), ((8, 6 * ROWS), F32),
         ((8, 128), F32), block, block, block, ((3 * ROWS, width), F32), ((3 * ROWS, width), F32)),
        8.0, 26, scalars, i0, ia, ib, t0, t1, s0, t0x, t1x, s0x, scratch=(pltpu.VMEM((3 * ROWS, 6 * ROWS), BF16),))
    s1, i2, loss = together(s1, i2, loss)
    sx = swap_cores(s1)
    loss, by_near_text, by_near_image, by_far_text, by_far_image, four, pair = call(
        far,
        (((8, 128), F32), ((ROWS, 6 * ROWS), BF16), ((ROWS, 6 * ROWS), BF16), ((4 * ROWS, 2 * ROWS), BF16),
         ((4 * ROWS, 2 * ROWS), BF16), ((4 * ROWS, width), BF16), ((2 * ROWS, width), BF16)),
        2.0, 16, scalars, i2, s1, sx, images, texts, image_inverse, text_inverse, loss)
    loss_c = swap_cores(loss)
    own_text, own_image, blocks = call(
        sums, (block, block, ((13 * ROWS, width), F32)), 4.0, 28, core,
        by_near_text, by_near_image, by_far_text, by_far_image, i2, four, pair, texts, ht0, ht1, hs0, htx, hi)
    loss = loss + loss_c
    blocks, loss = together(blocks, loss)
    other = swap_cores(narrow(blocks[:7 * ROWS]))
    loss = loss + move(loss, inner)
    other, loss = together(other, loss)
    own_text = own_text + widen(other[:ROWS])
    outs = [
        narrow(blocks[n * ROWS:(n + 2) * ROWS] + widen(other[(n - 6) * ROWS:(n - 4) * ROWS])) for n in (7, 9, 11)]
    back = (
        move(outs[0], inner, down),
        move(outs[1], outer_back, up),
        move(outs[2], far_back, across))
    loss, = call(everyone, (((64, 128), F32),), 20.0, 8, loss)
    loss = lax.all_to_all(loss, ("z", "xh", "y"), 0, 0, tiled=True)
    *back, loss = together(*back, loss)
    back = sum(widen(part) for part in back)
    stay = jnp.where(first, back[:ROWS], back[ROWS:])
    swapped = widen(swap_cores(narrow(jnp.where(first, back[ROWS:], back[:ROWS]))))
    text_hat = own_text + jnp.where(first, stay, swapped)
    image_hat = own_image + jnp.where(first, swapped, stay)
    image_grad, = call(finish, (block,), 20.0, 8, scalars, image_embed, image_hat)
    text_grad, loss = call(finish, (block, ((1,), F32)), 20.0, 8, scalars, text_embed, text_hat, loss)
    return loss, image_grad, text_grad


def solution(mesh):
    grid = Mesh(mesh.devices.reshape(SHAPE), AXES)
    rows = P(AXES, None)
    return jax.shard_map(
        body, mesh=grid, in_specs=(rows, rows, P(), P()), out_specs=(P(), rows, rows), check_vma=False)
```

```python
import jax
import jax.numpy as jnp
from jax import lax
from jax.experimental import pallas as pl
from jax.experimental.pallas import tpu as pltpu
from jax.sharding import Mesh, PartitionSpec as P

STEPS = 2
ROWS = 128
TILE = 256
AXES = ("z", "xh", "xl", "y", "c")
SHAPE = (8, 2, 2, 4, 2)
VMEM = pl.BlockSpec(memory_space=pltpu.VMEM)
SMEM = pl.BlockSpec(memory_space=pltpu.SMEM)
F32 = jnp.float32
BF16 = jnp.bfloat16


def call(kernel, outs, cost, limit, *args, scratch=()):
    shapes = tuple(jax.ShapeDtypeStruct(shape, dtype) for shape, dtype in outs)
    return pl.pallas_call(
        kernel,
        out_shape=shapes,
        in_specs=[SMEM if a.ndim == 1 else VMEM for a in args],
        out_specs=tuple(SMEM if len(s.shape) == 1 else VMEM for s in shapes),
        scratch_shapes=list(scratch),
        compiler_params=pltpu.CompilerParams(vmem_limit_bytes=limit * 2**20),
        cost_estimate=pl.CostEstimate(flops=int(cost * 1.0e9), bytes_accessed=int(cost * 3.0e6), transcendentals=0),
        name=kernel.__name__,
    )(*args)


def inverse_norm(rows):
    values = rows.astype(F32)
    return 1.0 / jnp.sqrt(jnp.sum(values * values, axis=1, keepdims=True) + 1e-06)


def as_row(column):
    eye = lax.broadcasted_iota(jnp.int32, (ROWS, ROWS), 0) == lax.broadcasted_iota(jnp.int32, (ROWS, ROWS), 1)
    parts = [
        jnp.sum(jnp.where(eye, column[n:n + ROWS], 0.0), axis=0, keepdims=True)
        for n in range(0, column.shape[0], ROWS)]
    return jnp.concatenate(parts, axis=1) if len(parts) > 1 else parts[0]


def dot_t(a, b):
    return lax.dot_general(a, b, (((1,), (1,)), ((), ())), preferred_element_type=F32)


def t_dot(a, b):
    return lax.dot_general(a, b, (((0,), (0,)), ((), ())), preferred_element_type=F32)


def dot(a, b):
    return jnp.dot(a, b, preferred_element_type=F32)


def terms(scalar_ref, products, image_inverse, text_inverse, own=False):
    z = products * (scalar_ref[0] * image_inverse) * text_inverse + scalar_ref[1]
    if own:
        row = lax.broadcasted_iota(jnp.int32, z.shape, 0)
        positive = (row == lax.broadcasted_iota(jnp.int32, z.shape, 1)) & (row < ROWS)
        z = jnp.where(positive, -z, z)
    small = jnp.exp(-jnp.abs(z))
    term = jnp.maximum(z, 0.0) + jnp.log1p(small)
    coef = jnp.where(z >= 0.0, 1.0, small) / (1.0 + small)
    if own:
        coef = jnp.where(positive, -coef, coef)
    total = sum(
        jnp.sum(term[:, n:n + 128].reshape(-1, 8, 128), axis=0) for n in range(0, z.shape[1], 128))
    return total, (coef * text_inverse).astype(BF16), (coef * image_inverse).astype(BF16)


def near(scalar_ref, i0, ia, ib, t0, t1, s0, t0x, t1x, s0x,
         images, texts, image_inverse, text_inverse, loss, ht0, ht1, hs0, htx, hi, coefs):
    for n, ref in enumerate((i0, ia, ib)):
        images[pl.ds(n * ROWS, ROWS), :] = ref[...]
    for n, ref in enumerate((t0, t1, s0, t0x, t1x, s0x)):
        texts[pl.ds(n * ROWS, ROWS), :] = ref[...]
    column = inverse_norm(images[...])
    image_inverse[...] = jnp.broadcast_to(column, image_inverse.shape)
    total = jnp.zeros((8, 128), F32)
    outs = (ht0, ht1, hs0)
    for tile in range(3):
        span = pl.ds(tile * TILE, TILE)
        block = texts[span, :]
        row = as_row(inverse_norm(block))
        text_inverse[:, span] = jnp.broadcast_to(row, (8, TILE))
        part, by_text, by_image = terms(scalar_ref, dot_t(images[...], block), column, row, own=tile == 0)
        total = total + part
        coefs[:, span] = by_text
        update = t_dot(by_image, images[...])
        for half in range(2):
            n = 2 * tile + half
            piece = update[half * ROWS:(half + 1) * ROWS]
            if n < 3:
                outs[n][...] = piece
            else:
                htx[pl.ds((n - 3) * ROWS, ROWS), :] = piece
    hi[...] = dot(coefs[...], texts[...])
    loss[...] = total


def far(scalar_ref, i2, s1, sx, images, texts, image_inverse, text_inverse, loss_in,
        loss, by_near_text, by_near_image, by_far_text, by_far_image, four, pair):
    four[pl.ds(0, 3 * ROWS), :] = images[...]
    four[pl.ds(3 * ROWS, ROWS), :] = i2[...]
    pair[pl.ds(0, ROWS), :] = s1[...]
    pair[pl.ds(ROWS, ROWS), :] = sx[...]
    column = inverse_norm(i2[...])
    total, by_text, by_image = terms(scalar_ref, dot_t(i2[...], texts[...]), column, text_inverse[0:1, :])
    by_near_text[...] = by_text
    by_near_image[...] = by_image
    columns = jnp.concatenate([image_inverse[:, 0:1], column], axis=0)
    part, by_text, by_image = terms(
        scalar_ref, dot_t(four[...], pair[...]), columns, as_row(inverse_norm(pair[...])))
    by_far_text[...] = by_text
    by_far_image[...] = by_image
    loss[...] = loss_in[...] + total + part


def sums(core_ref, by_near_text, by_near_image, by_far_text, by_far_image, i2, four, pair, texts,
         ht0, ht1, hs0, htx, hi, own_text, own_image, blocks):
    second = core_ref[0]

    def put(on_first, on_second, value):
        at = pl.multiple_of((on_first + (on_second - on_first) * second) * ROWS, ROWS)
        blocks[pl.ds(at, ROWS), :] = value

    for n, old in enumerate((ht0, ht1, hs0)):
        value = old[...] + t_dot(by_near_image[:, n * ROWS:(n + 1) * ROWS], i2[...])
        if n == 0:
            own_text[...] = value
        else:
            put(7 + 2 * (n - 1), 1 + 2 * (n - 1) + 1, value)
    for n in range(3):
        value = htx[pl.ds(n * ROWS, ROWS), :] + t_dot(
            by_near_image[:, (n + 3) * ROWS:(n + 4) * ROWS], i2[...])
        if n == 0:
            blocks[pl.ds(0, ROWS), :] = value
        else:
            put(7 + 2 * (n - 1) + 1, 1 + 2 * (n - 1), value)
    value = t_dot(by_far_image[...], four[...])
    put(11, 6, value[:ROWS])
    put(12, 5, value[ROWS:])
    for n in range(3):
        put(2 + 2 * n, 7 + 2 * n, jnp.zeros_like(own_text))
    rest = dot(by_far_text[...], pair[...])
    own_image[...] = hi[pl.ds(0, ROWS), :] + rest[:ROWS]
    for n in (1, 2):
        put(2 * n - 1, 6 + 2 * n, hi[pl.ds(n * ROWS, ROWS), :] + rest[n * ROWS:(n + 1) * ROWS])
    put(5, 12, dot(by_near_text[...], texts[...]) + rest[3 * ROWS:])


def everyone(loss, out):
    out[...] = jnp.broadcast_to(jnp.sum(loss[...], axis=0, keepdims=True), out.shape)


def finish(scalar_ref, image, text, image_hat, text_hat, parts, image_grad, text_grad, loss):
    for raw, hat_ref, out in ((image, image_hat, image_grad), (text, text_hat, text_grad)):
        inverse = inverse_norm(raw[...])
        unit = raw[...].astype(F32) * inverse
        hat = scalar_ref[0] * hat_ref[...]
        out[...] = (hat - unit * jnp.sum(unit * hat, axis=1, keepdims=True)) * inverse
    loss[0] = jnp.sum(parts[...]) / (ROWS * 256 * STEPS * ROWS * 16)


def inner(group, side, y):
    return group, 1 - side, y


def outer(group, side, y):
    return (group + 1) % 16, 1 - side, y


def outer_back(group, side, y):
    return (group + 15) % 16, 1 - side, y


def far_back(group, side, y):
    return (group + 15) % 16, side, y


def up(group, side, y):
    return group, side, (y + 1) % 4


def down(group, side, y):
    return group, side, (y + 3) % 4


def across(group, side, y):
    return group, side, (y + 2) % 4


def move(block, first, second=None):
    route = []
    for chip in range(128):
        place = (chip // 8, chip // 4 % 2, chip % 4)
        for core, to in enumerate((first, second or first)):
            group, side, y = to(*place)
            route.append((chip * 2 + core, (group * 8 + side * 4 + y) * 2 + core))
    return lax.ppermute(block, AXES, route)


def swap_cores(block):
    return lax.ppermute(block, "c", [(0, 1), (1, 0)])


def narrow(block):
    return (block * 32.0).astype(jnp.float16)


def widen(block):
    return block.astype(F32) * (1.0 / 32.0)


def together(*arrays):
    return lax.optimization_barrier(arrays)


def body(image_embed, text_embed, log_scale, logit_bias):
    width = image_embed.shape[1]
    scalars = jnp.stack([jnp.exp(log_scale[0]), logit_bias[0]])
    core = jnp.reshape(lax.axis_index("c"), (1,))
    first = lax.axis_index("c") == 0
    i0, t0 = image_embed, text_embed
    block = ((ROWS, width), F32)

    s0, t1 = move(t0, outer), move(t0, inner)
    ia, ib, t0x = move(i0, up), move(i0, down), swap_cores(t0)
    s0x, t1x = swap_cores(s0), swap_cores(t1)
    s0, t1 = together(s0, t1)
    s1 = move(jnp.where(first, t1, s0), outer, inner)
    ia, ib, t0x, s0x, t1x = together(ia, ib, t0x, s0x, t1x)
    i2 = move(jnp.where(first, ia, ib), up, down)
    images, texts, image_inverse, text_inverse, loss, ht0, ht1, hs0, htx, hi = call(
        near,
        (((3 * ROWS, width), BF16), ((6 * ROWS, width), BF16), ((3 * ROWS, 128), F32), ((8, 6 * ROWS), F32),
         ((8, 128), F32), block, block, block, ((3 * ROWS, width), F32), ((3 * ROWS, width), F32)),
        8.0, 26, scalars, i0, ia, ib, t0, t1, s0, t0x, t1x, s0x, scratch=(pltpu.VMEM((3 * ROWS, 6 * ROWS), BF16),))
    s1, i2, loss = together(s1, i2, loss)
    sx = swap_cores(s1)
    loss, by_near_text, by_near_image, by_far_text, by_far_image, four, pair = call(
        far,
        (((8, 128), F32), ((ROWS, 6 * ROWS), BF16), ((ROWS, 6 * ROWS), BF16), ((4 * ROWS, 2 * ROWS), BF16),
         ((4 * ROWS, 2 * ROWS), BF16), ((4 * ROWS, width), BF16), ((2 * ROWS, width), BF16)),
        2.0, 16, scalars, i2, s1, sx, images, texts, image_inverse, text_inverse, loss)
    loss_y = lax.ppermute(loss, "y", [(i, i ^ 1) for i in range(4)])
    own_text, own_image, blocks = call(
        sums, (block, block, ((13 * ROWS, width), F32)), 4.0, 28, core,
        by_near_text, by_near_image, by_far_text, by_far_image, i2, four, pair, texts, ht0, ht1, hs0, htx, hi)
    loss = loss + loss_y
    blocks, loss = together(blocks, loss)
    message = narrow(blocks[:7 * ROWS])
    other = swap_cores(message)
    loss = loss + move(loss, inner)
    other, loss = together(other, loss)
    loss = loss + lax.ppermute(loss, "y", [(i, i ^ 2) for i in range(4)])
    own_text = own_text + widen(other[:ROWS])
    outs = [
        narrow(blocks[n * ROWS:(n + 2) * ROWS] + widen(other[(n - 6) * ROWS:(n - 4) * ROWS])) for n in (7, 9, 11)]
    back = (
        move(outs[0], inner, down),
        move(outs[1], outer_back, up),
        move(outs[2], far_back, across))
    loss, = call(everyone, (((16, 128), F32),), 20.0, 4, loss)
    loss = lax.all_to_all(loss, ("z", "xh"), 0, 0, tiled=True)
    *back, loss = together(*back, loss)
    back = sum(widen(part) for part in back)
    stay = jnp.where(first, back[:ROWS], back[ROWS:])
    swapped = widen(swap_cores(narrow(jnp.where(first, back[ROWS:], back[:ROWS]))))
    loss = loss + swap_cores(loss)
    text_hat = own_text + jnp.where(first, stay, swapped)
    image_hat = own_image + jnp.where(first, swapped, stay)
    image_grad, text_grad, loss = call(
        finish, (block, block, ((1,), F32)), 20.0, 12, scalars, image_embed, text_embed, image_hat, text_hat, loss)
    return loss, image_grad, text_grad


def solution(mesh):
    grid = Mesh(mesh.devices.reshape(SHAPE), AXES)
    rows = P(AXES, None)
    return jax.shard_map(
        body, mesh=grid, in_specs=(rows, rows, P(), P()), out_specs=(P(), rows, rows), check_vma=False)
```

```python
import jax
import jax.numpy as jnp
from jax import lax
from jax.experimental import pallas as pl
from jax.experimental.pallas import tpu as pltpu
from jax.sharding import Mesh, PartitionSpec as P

STEPS = 2
ROWS = 128
TILE = 256
AXES = ("z", "xh", "xl", "y", "c")
SHAPE = (8, 2, 2, 4, 2)
VMEM = pl.BlockSpec(memory_space=pltpu.VMEM)
SMEM = pl.BlockSpec(memory_space=pltpu.SMEM)
F32 = jnp.float32
BF16 = jnp.bfloat16


def call(kernel, outs, cost, limit, *args, scratch=()):
    shapes = tuple(jax.ShapeDtypeStruct(shape, dtype) for shape, dtype in outs)
    return pl.pallas_call(
        kernel,
        out_shape=shapes,
        in_specs=[SMEM if a.ndim == 1 else VMEM for a in args],
        out_specs=tuple(SMEM if len(s.shape) == 1 else VMEM for s in shapes),
        scratch_shapes=list(scratch),
        compiler_params=pltpu.CompilerParams(vmem_limit_bytes=limit * 2**20),
        cost_estimate=pl.CostEstimate(flops=int(cost * 1.0e9), bytes_accessed=int(cost * 3.0e6), transcendentals=0),
        name=kernel.__name__,
    )(*args)


def inverse_norm(rows):
    values = rows.astype(F32)
    return 1.0 / jnp.sqrt(jnp.sum(values * values, axis=1, keepdims=True) + 1e-06)


def as_row(column):
    eye = lax.broadcasted_iota(jnp.int32, (ROWS, ROWS), 0) == lax.broadcasted_iota(jnp.int32, (ROWS, ROWS), 1)
    parts = [
        jnp.sum(jnp.where(eye, column[n:n + ROWS], 0.0), axis=0, keepdims=True)
        for n in range(0, column.shape[0], ROWS)]
    return jnp.concatenate(parts, axis=1) if len(parts) > 1 else parts[0]


def dot_t(a, b):
    return lax.dot_general(a, b, (((1,), (1,)), ((), ())), preferred_element_type=F32)


def t_dot(a, b):
    return lax.dot_general(a, b, (((0,), (0,)), ((), ())), preferred_element_type=F32)


def dot(a, b):
    return jnp.dot(a, b, preferred_element_type=F32)


def terms(scalar_ref, products, image_inverse, text_inverse, own=False):
    z = products * (scalar_ref[0] * image_inverse) * text_inverse + scalar_ref[1]
    if own:
        row = lax.broadcasted_iota(jnp.int32, z.shape, 0)
        positive = (row == lax.broadcasted_iota(jnp.int32, z.shape, 1)) & (row < ROWS)
        z = jnp.where(positive, -z, z)
    small = jnp.exp(-jnp.abs(z))
    term = jnp.maximum(z, 0.0) + jnp.log1p(small)
    coef = jnp.where(z >= 0.0, 1.0, small) / (1.0 + small)
    if own:
        coef = jnp.where(positive, -coef, coef)
    total = sum(
        jnp.sum(term[:, n:n + 128].reshape(-1, 8, 128), axis=0) for n in range(0, z.shape[1], 128))
    return total, (coef * text_inverse).astype(BF16), (coef * image_inverse).astype(BF16)


def near(scalar_ref, i0, ia, ib, t0, t1, s0, t0x, t1x, s0x,
         images, texts, image_inverse, text_inverse, loss, by_text, by_image):
    for n, ref in enumerate((i0, ia, ib)):
        images[pl.ds(n * ROWS, ROWS), :] = ref[...]
    for n, ref in enumerate((t0, t1, s0, t0x, t1x, s0x)):
        texts[pl.ds(n * ROWS, ROWS), :] = ref[...]
    column = inverse_norm(images[...])
    image_inverse[...] = jnp.broadcast_to(column, image_inverse.shape)
    total = jnp.zeros((8, 128), F32)
    for tile in range(3):
        span = pl.ds(tile * TILE, TILE)
        block = texts[span, :]
        row = as_row(inverse_norm(block))
        text_inverse[:, span] = jnp.broadcast_to(row, (8, TILE))
        part, by_text[:, span], by_image[:, span] = terms(
            scalar_ref, dot_t(images[...], block), column, row, own=tile == 0)
        total = total + part
    loss[...] = total


def near_sums(by_text, by_image, images, texts, ht0, ht1, hs0, htx, hi):
    outs = (ht0, ht1, hs0)
    for tile in range(3):
        update = t_dot(by_image[:, tile * TILE:(tile + 1) * TILE], images[...])
        for half in range(2):
            n = 2 * tile + half
            piece = update[half * ROWS:(half + 1) * ROWS]
            if n < 3:
                outs[n][...] = piece
            else:
                htx[pl.ds((n - 3) * ROWS, ROWS), :] = piece
    hi[...] = dot(by_text[...], texts[...])


def far(scalar_ref, i2, s1, sx, images, texts, image_inverse, text_inverse, loss_in,
        loss, by_near_text, by_near_image, by_far_text, by_far_image, four, pair):
    four[pl.ds(0, 3 * ROWS), :] = images[...]
    four[pl.ds(3 * ROWS, ROWS), :] = i2[...]
    pair[pl.ds(0, ROWS), :] = s1[...]
    pair[pl.ds(ROWS, ROWS), :] = sx[...]
    column = inverse_norm(i2[...])
    total, by_text, by_image = terms(scalar_ref, dot_t(i2[...], texts[...]), column, text_inverse[0:1, :])
    by_near_text[...] = by_text
    by_near_image[...] = by_image
    columns = jnp.concatenate([image_inverse[:, 0:1], column], axis=0)
    part, by_text, by_image = terms(
        scalar_ref, dot_t(four[...], pair[...]), columns, as_row(inverse_norm(pair[...])))
    by_far_text[...] = by_text
    by_far_image[...] = by_image
    loss[...] = loss_in[...] + total + part


def sums(core_ref, by_near_text, by_near_image, by_far_text, by_far_image, i2, four, pair, texts,
         ht0, ht1, hs0, htx, hi, own_text, own_image, blocks):
    second = core_ref[0]

    def put(on_first, on_second, value):
        at = pl.multiple_of((on_first + (on_second - on_first) * second) * ROWS, ROWS)
        blocks[pl.ds(at, ROWS), :] = value

    for n, old in enumerate((ht0, ht1, hs0)):
        value = old[...] + t_dot(by_near_image[:, n * ROWS:(n + 1) * ROWS], i2[...])
        if n == 0:
            own_text[...] = value
        else:
            put(7 + 2 * (n - 1), 1 + 2 * (n - 1) + 1, value)
    for n in range(3):
        value = htx[pl.ds(n * ROWS, ROWS), :] + t_dot(
            by_near_image[:, (n + 3) * ROWS:(n + 4) * ROWS], i2[...])
        if n == 0:
            blocks[pl.ds(0, ROWS), :] = value
        else:
            put(7 + 2 * (n - 1) + 1, 1 + 2 * (n - 1), value)
    value = t_dot(by_far_image[...], four[...])
    put(11, 6, value[:ROWS])
    put(12, 5, value[ROWS:])
    for n in range(3):
        put(2 + 2 * n, 7 + 2 * n, jnp.zeros_like(own_text))
    rest = dot(by_far_text[...], pair[...])
    own_image[...] = hi[pl.ds(0, ROWS), :] + rest[:ROWS]
    for n in (1, 2):
        put(2 * n - 1, 6 + 2 * n, hi[pl.ds(n * ROWS, ROWS), :] + rest[n * ROWS:(n + 1) * ROWS])
    put(5, 12, dot(by_near_text[...], texts[...]) + rest[3 * ROWS:])


def everyone(loss, out):
    out[...] = jnp.broadcast_to(jnp.sum(loss[...], axis=0, keepdims=True), out.shape)


def finish(scalar_ref, image, text, image_hat, text_hat, parts, image_grad, text_grad, loss):
    for raw, hat_ref, out in ((image, image_hat, image_grad), (text, text_hat, text_grad)):
        inverse = inverse_norm(raw[...])
        unit = raw[...].astype(F32) * inverse
        hat = scalar_ref[0] * hat_ref[...]
        out[...] = (hat - unit * jnp.sum(unit * hat, axis=1, keepdims=True)) * inverse
    loss[0] = jnp.sum(parts[...]) / (ROWS * 256 * STEPS * ROWS * 16)


def inner(group, side, y):
    return group, 1 - side, y


def outer(group, side, y):
    return (group + 1) % 16, 1 - side, y


def outer_back(group, side, y):
    return (group + 15) % 16, 1 - side, y


def far_back(group, side, y):
    return (group + 15) % 16, side, y


def up(group, side, y):
    return group, side, (y + 1) % 4


def down(group, side, y):
    return group, side, (y + 3) % 4


def across(group, side, y):
    return group, side, (y + 2) % 4


def move(block, first, second=None):
    route = []
    for chip in range(128):
        place = (chip // 8, chip // 4 % 2, chip % 4)
        for core, to in enumerate((first, second or first)):
            group, side, y = to(*place)
            route.append((chip * 2 + core, (group * 8 + side * 4 + y) * 2 + core))
    return lax.ppermute(block, AXES, route)


def swap_cores(block):
    return lax.ppermute(block, "c", [(0, 1), (1, 0)])


def narrow(block):
    return (block * 32.0).astype(jnp.float16)


def widen(block):
    return block.astype(F32) * (1.0 / 32.0)


def together(*arrays):
    return lax.optimization_barrier(arrays)


def body(image_embed, text_embed, log_scale, logit_bias):
    width = image_embed.shape[1]
    scalars = jnp.stack([jnp.exp(log_scale[0]), logit_bias[0]])
    core = jnp.reshape(lax.axis_index("c"), (1,))
    first = lax.axis_index("c") == 0
    i0, t0 = image_embed, text_embed
    block = ((ROWS, width), F32)

    s0, t1 = move(t0, outer), move(t0, inner)
    ia, ib, t0x = move(i0, up), move(i0, down), swap_cores(t0)
    s0, t1 = together(s0, t1)
    s1 = move(jnp.where(first, t1, s0), outer, inner)
    ia, ib, t0x, t1, s0 = together(ia, ib, t0x, t1, s0)
    i2 = move(jnp.where(first, ia, ib), up, down)
    s0x, t1x = swap_cores(s0), swap_cores(t1)
    pairs = ((3 * ROWS, 6 * ROWS), BF16)
    images, texts, image_inverse, text_inverse, loss, near_by_text, near_by_image = call(
        near,
        (((3 * ROWS, width), BF16), ((6 * ROWS, width), BF16), ((3 * ROWS, 128), F32), ((8, 6 * ROWS), F32),
         ((8, 128), F32), pairs, pairs),
        8.0, 20, scalars, i0, ia, ib, t0, t1, s0, t0x, t1x, s0x)
    s1, loss = together(s1, loss)
    sx = swap_cores(s1)
    ht0, ht1, hs0, htx, hi = call(
        near_sums, (block, block, block, ((3 * ROWS, width), F32), ((3 * ROWS, width), F32)), 4.0, 20,
        near_by_text, near_by_image, images, texts)
    loss, by_near_text, by_near_image, by_far_text, by_far_image, four, pair = call(
        far,
        (((8, 128), F32), ((ROWS, 6 * ROWS), BF16), ((ROWS, 6 * ROWS), BF16), ((4 * ROWS, 2 * ROWS), BF16),
         ((4 * ROWS, 2 * ROWS), BF16), ((4 * ROWS, width), BF16), ((2 * ROWS, width), BF16)),
        2.0, 16, scalars, i2, s1, sx, images, texts, image_inverse, text_inverse, loss)
    loss_y = lax.ppermute(loss, "y", [(i, i ^ 1) for i in range(4)])
    own_text, own_image, blocks = call(
        sums, (block, block, ((13 * ROWS, width), F32)), 4.0, 28, core,
        by_near_text, by_near_image, by_far_text, by_far_image, i2, four, pair, texts, ht0, ht1, hs0, htx, hi)
    loss = loss + loss_y
    blocks, loss = together(blocks, loss)
    message = narrow(blocks[:7 * ROWS])
    other = swap_cores(message)
    loss = loss + move(loss, inner)
    other, loss = together(other, loss)
    loss = loss + lax.ppermute(loss, "y", [(i, i ^ 2) for i in range(4)])
    own_text = own_text + widen(other[:ROWS])
    outs = [
        narrow(blocks[n * ROWS:(n + 2) * ROWS] + widen(other[(n - 6) * ROWS:(n - 4) * ROWS])) for n in (7, 9, 11)]
    back = (
        move(outs[0], inner, down),
        move(outs[1], outer_back, up),
        move(outs[2], far_back, across))
    loss, = call(everyone, (((32, 128), F32),), 20.0, 4, loss)
    loss = lax.all_to_all(loss, ("z", "xh", "c"), 0, 0, tiled=True)
    *back, loss = together(*back, loss)
    back = sum(widen(part) for part in back)
    stay = jnp.where(first, back[:ROWS], back[ROWS:])
    swapped = widen(swap_cores(narrow(jnp.where(first, back[ROWS:], back[:ROWS]))))
    text_hat = own_text + jnp.where(first, stay, swapped)
    image_hat = own_image + jnp.where(first, swapped, stay)
    image_grad, text_grad, loss = call(
        finish, (block, block, ((1,), F32)), 20.0, 12, scalars, image_embed, text_embed, image_hat, text_hat, loss)
    return loss, image_grad, text_grad


def solution(mesh):
    grid = Mesh(mesh.devices.reshape(SHAPE), AXES)
    rows = P(AXES, None)
    return jax.shard_map(
        body, mesh=grid, in_specs=(rows, rows, P(), P()), out_specs=(P(), rows, rows), check_vma=False)
```

```python
import jax
import jax.numpy as jnp
from jax import lax
from jax.experimental import pallas as pl
from jax.experimental.pallas import tpu as pltpu
from jax.sharding import Mesh, PartitionSpec as P

STEPS = 2
ROWS = 128
TILE = 256
AXES = ("z", "xh", "xl", "y", "c")
SHAPE = (8, 2, 2, 4, 2)
VMEM = pl.BlockSpec(memory_space=pltpu.VMEM)
SMEM = pl.BlockSpec(memory_space=pltpu.SMEM)
F32 = jnp.float32
BF16 = jnp.bfloat16


def call(kernel, outs, cost, limit, *args, scratch=()):
    shapes = tuple(jax.ShapeDtypeStruct(shape, dtype) for shape, dtype in outs)
    return pl.pallas_call(
        kernel,
        out_shape=shapes,
        in_specs=[SMEM if a.ndim == 1 else VMEM for a in args],
        out_specs=tuple(SMEM if len(s.shape) == 1 else VMEM for s in shapes),
        scratch_shapes=list(scratch),
        compiler_params=pltpu.CompilerParams(vmem_limit_bytes=limit * 2**20),
        cost_estimate=pl.CostEstimate(flops=int(cost * 1.0e9), bytes_accessed=int(cost * 3.0e6), transcendentals=0),
        name=kernel.__name__,
    )(*args)


def inverse_norm(rows):
    values = rows.astype(F32)
    return 1.0 / jnp.sqrt(jnp.sum(values * values, axis=1, keepdims=True) + 1e-06)


def as_row(column):
    eye = lax.broadcasted_iota(jnp.int32, (ROWS, ROWS), 0) == lax.broadcasted_iota(jnp.int32, (ROWS, ROWS), 1)
    parts = [
        jnp.sum(jnp.where(eye, column[n:n + ROWS], 0.0), axis=0, keepdims=True)
        for n in range(0, column.shape[0], ROWS)]
    return jnp.concatenate(parts, axis=1) if len(parts) > 1 else parts[0]


def dot_t(a, b):
    return lax.dot_general(a, b, (((1,), (1,)), ((), ())), preferred_element_type=F32)


def t_dot(a, b):
    return lax.dot_general(a, b, (((0,), (0,)), ((), ())), preferred_element_type=F32)


def dot(a, b):
    return jnp.dot(a, b, preferred_element_type=F32)


def terms(scalar_ref, products, image_inverse, text_inverse, own=False):
    z = products * (scalar_ref[0] * image_inverse) * text_inverse + scalar_ref[1]
    if own:
        row = lax.broadcasted_iota(jnp.int32, z.shape, 0)
        positive = (row == lax.broadcasted_iota(jnp.int32, z.shape, 1)) & (row < ROWS)
        z = jnp.where(positive, -z, z)
    small = jnp.exp(-jnp.abs(z))
    term = jnp.maximum(z, 0.0) + jnp.log1p(small)
    coef = jnp.where(z >= 0.0, 1.0, small) / (1.0 + small)
    if own:
        coef = jnp.where(positive, -coef, coef)
    total = sum(
        jnp.sum(term[:, n:n + 128].reshape(-1, 8, 128), axis=0) for n in range(0, z.shape[1], 128))
    return total, (coef * text_inverse).astype(BF16), (coef * image_inverse).astype(BF16)


def near(scalar_ref, i0, ia, ib, t0, t1, s0, t0x, t1x, s0x,
         images, texts, image_inverse, text_inverse, loss, by_text, by_image):
    for n, ref in enumerate((i0, ia, ib)):
        images[pl.ds(n * ROWS, ROWS), :] = ref[...]
    for n, ref in enumerate((t0, t1, s0, t0x, t1x, s0x)):
        texts[pl.ds(n * ROWS, ROWS), :] = ref[...]
    column = inverse_norm(images[...])
    image_inverse[...] = jnp.broadcast_to(column, image_inverse.shape)
    total = jnp.zeros((8, 128), F32)
    for tile in range(3):
        span = pl.ds(tile * TILE, TILE)
        block = texts[span, :]
        row = as_row(inverse_norm(block))
        text_inverse[:, span] = jnp.broadcast_to(row, (8, TILE))
        part, by_text[:, span], by_image[:, span] = terms(
            scalar_ref, dot_t(images[...], block), column, row, own=tile == 0)
        total = total + part
    loss[...] = total


def near_sums(by_text, by_image, images, texts, ht1, hs0, htx, hi):
    update = t_dot(by_image[:, ROWS:3 * ROWS], images[...])
    ht1[...] = update[:ROWS]
    hs0[...] = update[ROWS:]
    htx[...] = t_dot(by_image[:, 3 * ROWS:], images[...])
    hi[...] = dot(by_text[pl.ds(ROWS, 2 * ROWS), :], texts[...])


def own_sums(near_by_text, near_by_image, by_near_image, by_far_text, images, texts, i2, pair, own_text, own_image):
    own_text[...] = t_dot(near_by_image[:, :ROWS], images[...]) + t_dot(by_near_image[:, :ROWS], i2[...])
    own_image[...] = dot(near_by_text[pl.ds(0, ROWS), :], texts[...]) + dot(by_far_text[pl.ds(0, ROWS), :], pair[...])


def far(scalar_ref, i2, s1, sx, images, texts, image_inverse, text_inverse, loss_in,
        loss, by_near_text, by_near_image, by_far_text, by_far_image, four, pair):
    four[pl.ds(0, 3 * ROWS), :] = images[...]
    four[pl.ds(3 * ROWS, ROWS), :] = i2[...]
    pair[pl.ds(0, ROWS), :] = s1[...]
    pair[pl.ds(ROWS, ROWS), :] = sx[...]
    column = inverse_norm(i2[...])
    total, by_text, by_image = terms(scalar_ref, dot_t(i2[...], texts[...]), column, text_inverse[0:1, :])
    by_near_text[...] = by_text
    by_near_image[...] = by_image
    columns = jnp.concatenate([image_inverse[:, 0:1], column], axis=0)
    part, by_text, by_image = terms(
        scalar_ref, dot_t(four[...], pair[...]), columns, as_row(inverse_norm(pair[...])))
    by_far_text[...] = by_text
    by_far_image[...] = by_image
    loss[...] = loss_in[...] + total + part


def sums(core_ref, by_near_text, by_near_image, by_far_text, by_far_image, i2, four, pair, texts,
         ht1, hs0, htx, hi, blocks):
    second = core_ref[0]

    def put(on_first, on_second, value):
        at = pl.multiple_of((on_first + (on_second - on_first) * second) * ROWS, ROWS)
        blocks[pl.ds(at, ROWS), :] = value

    for n, old in ((1, ht1), (2, hs0)):
        value = old[...] + t_dot(by_near_image[:, n * ROWS:(n + 1) * ROWS], i2[...])
        put(7 + 2 * (n - 1), 1 + 2 * (n - 1) + 1, value)
    for n in range(3):
        value = htx[pl.ds(n * ROWS, ROWS), :] + t_dot(
            by_near_image[:, (n + 3) * ROWS:(n + 4) * ROWS], i2[...])
        if n == 0:
            blocks[pl.ds(0, ROWS), :] = value
        else:
            put(7 + 2 * (n - 1) + 1, 1 + 2 * (n - 1), value)
    value = t_dot(by_far_image[...], four[...])
    put(11, 6, value[:ROWS])
    put(12, 5, value[ROWS:])
    for n in range(3):
        put(2 + 2 * n, 7 + 2 * n, jnp.zeros_like(i2, dtype=F32))
    rest = dot(by_far_text[pl.ds(ROWS, 3 * ROWS), :], pair[...])
    for n in (1, 2):
        put(2 * n - 1, 6 + 2 * n, hi[pl.ds((n - 1) * ROWS, ROWS), :] + rest[(n - 1) * ROWS:n * ROWS])
    put(5, 12, dot(by_near_text[...], texts[...]) + rest[2 * ROWS:])


def everyone(loss, out):
    out[...] = jnp.broadcast_to(jnp.sum(loss[...], axis=0, keepdims=True), out.shape)


def finish(scalar_ref, image, text, image_hat, text_hat, parts, image_grad, text_grad, loss):
    for raw, hat_ref, out in ((image, image_hat, image_grad), (text, text_hat, text_grad)):
        inverse = inverse_norm(raw[...])
        unit = raw[...].astype(F32) * inverse
        hat = scalar_ref[0] * hat_ref[...]
        out[...] = (hat - unit * jnp.sum(unit * hat, axis=1, keepdims=True)) * inverse
    loss[0] = jnp.sum(parts[...]) / (ROWS * 256 * STEPS * ROWS * 16)


def inner(group, side, y):
    return group, 1 - side, y


def outer(group, side, y):
    return (group + 1) % 16, 1 - side, y


def outer_back(group, side, y):
    return (group + 15) % 16, 1 - side, y


def far_back(group, side, y):
    return (group + 15) % 16, side, y


def up(group, side, y):
    return group, side, (y + 1) % 4


def down(group, side, y):
    return group, side, (y + 3) % 4


def across(group, side, y):
    return group, side, (y + 2) % 4


def move(block, first, second=None):
    route = []
    for chip in range(128):
        place = (chip // 8, chip // 4 % 2, chip % 4)
        for core, to in enumerate((first, second or first)):
            group, side, y = to(*place)
            route.append((chip * 2 + core, (group * 8 + side * 4 + y) * 2 + core))
    return lax.ppermute(block, AXES, route)


def swap_cores(block):
    return lax.ppermute(block, "c", [(0, 1), (1, 0)])


def narrow(block):
    return (block * 32.0).astype(jnp.float16)


def widen(block):
    return block.astype(F32) * (1.0 / 32.0)


def together(*arrays):
    return lax.optimization_barrier(arrays)


def body(image_embed, text_embed, log_scale, logit_bias):
    width = image_embed.shape[1]
    scalars = jnp.stack([jnp.exp(log_scale[0]), logit_bias[0]])
    core = jnp.reshape(lax.axis_index("c"), (1,))
    first = lax.axis_index("c") == 0
    i0, t0 = image_embed, text_embed
    block = ((ROWS, width), F32)

    t1, s0 = move(t0, inner), move(t0, outer)
    ia, ib, t0x = move(i0, up), move(i0, down), swap_cores(t0)
    t1, s0 = together(t1, s0)
    s1 = move(jnp.where(first, t1, s0), outer, inner)
    ia, ib, t0x, t1, s0 = together(ia, ib, t0x, t1, s0)
    i2 = move(jnp.where(first, ia, ib), up, down)
    s0x, t1x = swap_cores(s0), swap_cores(t1)
    pairs = ((3 * ROWS, 6 * ROWS), BF16)
    images, texts, image_inverse, text_inverse, loss, near_by_text, near_by_image = call(
        near,
        (((3 * ROWS, width), BF16), ((6 * ROWS, width), BF16), ((3 * ROWS, 128), F32), ((8, 6 * ROWS), F32),
         ((8, 128), F32), pairs, pairs),
        8.0, 20, scalars, i0, ia, ib, t0, t1, s0, t0x, t1x, s0x)
    s1, loss = together(s1, loss)
    sx = swap_cores(s1)
    ht1, hs0, htx, hi = call(
        near_sums, (block, block, ((3 * ROWS, width), F32), ((2 * ROWS, width), F32)), 4.0, 20,
        near_by_text, near_by_image, images, texts)
    loss, by_near_text, by_near_image, by_far_text, by_far_image, four, pair = call(
        far,
        (((8, 128), F32), ((ROWS, 6 * ROWS), BF16), ((ROWS, 6 * ROWS), BF16), ((4 * ROWS, 2 * ROWS), BF16),
         ((4 * ROWS, 2 * ROWS), BF16), ((4 * ROWS, width), BF16), ((2 * ROWS, width), BF16)),
        2.0, 16, scalars, i2, s1, sx, images, texts, image_inverse, text_inverse, loss)
    loss_y = lax.ppermute(loss, "y", [(i, i ^ 1) for i in range(4)])
    blocks, = call(
        sums, (((13 * ROWS, width), F32),), 4.0, 28, core,
        by_near_text, by_near_image, by_far_text, by_far_image, i2, four, pair, texts, ht1, hs0, htx, hi)
    loss = loss + loss_y
    blocks, loss = together(blocks, loss)
    message = narrow(blocks[:7 * ROWS])
    other = swap_cores(message)
    loss = loss + move(loss, inner)
    own_text, own_image = call(
        own_sums, (block, block), 2.0, 20,
        near_by_text, near_by_image, by_near_image, by_far_text, images, texts, i2, pair)
    other, loss, own_text, own_image = together(other, loss, own_text, own_image)
    loss = loss + lax.ppermute(loss, "y", [(i, i ^ 2) for i in range(4)])
    own_text = own_text + widen(other[:ROWS])
    outs = [
        narrow(blocks[n * ROWS:(n + 2) * ROWS] + widen(other[(n - 6) * ROWS:(n - 4) * ROWS])) for n in (7, 9, 11)]
    back_far = move(outs[2], far_back, across)
    back_outer = move(outs[1], outer_back, up)
    back = (back_far, back_outer, move(outs[0], inner, down))
    loss, = call(everyone, (((32, 128), F32),), 20.0, 4, loss)
    loss = lax.all_to_all(loss, ("z", "xh", "c"), 0, 0, tiled=True)
    *back, loss = together(*back, loss)
    back = sum(widen(part) for part in back)
    stay = jnp.where(first, back[:ROWS], back[ROWS:])
    swapped = widen(swap_cores(narrow(jnp.where(first, back[ROWS:], back[:ROWS]))))
    text_hat = own_text + jnp.where(first, stay, swapped)
    image_hat = own_image + jnp.where(first, swapped, stay)
    image_grad, text_grad, loss = call(
        finish, (block, block, ((1,), F32)), 20.0, 12, scalars, image_embed, text_embed, image_hat, text_hat, loss)
    return loss, image_grad, text_grad


def solution(mesh):
    grid = Mesh(mesh.devices.reshape(SHAPE), AXES)
    rows = P(AXES, None)
    return jax.shard_map(
        body, mesh=grid, in_specs=(rows, rows, P(), P()), out_specs=(P(), rows, rows), check_vma=False)
```

```python
import jax
import jax.numpy as jnp
from jax import lax
from jax.experimental import pallas as pl
from jax.experimental.pallas import tpu as pltpu
from jax.sharding import Mesh, PartitionSpec as P

STEPS = 2
ROWS = 128
TILE = 256
AXES = ("z", "xh", "xl", "y", "c")
SHAPE = (8, 2, 2, 4, 2)
VMEM = pl.BlockSpec(memory_space=pltpu.VMEM)
SMEM = pl.BlockSpec(memory_space=pltpu.SMEM)
F32 = jnp.float32
BF16 = jnp.bfloat16


def call(kernel, outs, cost, limit, *args, scratch=()):
    shapes = tuple(jax.ShapeDtypeStruct(shape, dtype) for shape, dtype in outs)
    return pl.pallas_call(
        kernel,
        out_shape=shapes,
        in_specs=[SMEM if a.ndim == 1 else VMEM for a in args],
        out_specs=tuple(SMEM if len(s.shape) == 1 else VMEM for s in shapes),
        scratch_shapes=list(scratch),
        compiler_params=pltpu.CompilerParams(vmem_limit_bytes=limit * 2**20),
        cost_estimate=pl.CostEstimate(flops=int(cost * 1.0e9), bytes_accessed=int(cost * 3.0e6), transcendentals=0),
        name=kernel.__name__,
    )(*args)


def inverse_norm(rows):
    values = rows.astype(F32)
    return 1.0 / jnp.sqrt(jnp.sum(values * values, axis=1, keepdims=True) + 1e-06)


def as_row(column):
    eye = lax.broadcasted_iota(jnp.int32, (ROWS, ROWS), 0) == lax.broadcasted_iota(jnp.int32, (ROWS, ROWS), 1)
    parts = [
        jnp.sum(jnp.where(eye, column[n:n + ROWS], 0.0), axis=0, keepdims=True)
        for n in range(0, column.shape[0], ROWS)]
    return jnp.concatenate(parts, axis=1) if len(parts) > 1 else parts[0]


def dot_t(a, b):
    return lax.dot_general(a, b, (((1,), (1,)), ((), ())), preferred_element_type=F32)


def t_dot(a, b):
    return lax.dot_general(a, b, (((0,), (0,)), ((), ())), preferred_element_type=F32)


def dot(a, b):
    return jnp.dot(a, b, preferred_element_type=F32)


def terms(scalar_ref, products, image_inverse, text_inverse, own=False):
    z = products * (scalar_ref[0] * image_inverse) * text_inverse + scalar_ref[1]
    if own:
        row = lax.broadcasted_iota(jnp.int32, z.shape, 0)
        positive = (row == lax.broadcasted_iota(jnp.int32, z.shape, 1)) & (row < ROWS)
        z = jnp.where(positive, -z, z)
    small = jnp.exp(-jnp.abs(z))
    term = jnp.maximum(z, 0.0) + jnp.log1p(small)
    coef = jnp.where(z >= 0.0, 1.0, small) / (1.0 + small)
    if own:
        coef = jnp.where(positive, -coef, coef)
    total = sum(
        jnp.sum(term[:, n:n + 128].reshape(-1, 8, 128), axis=0) for n in range(0, z.shape[1], 128))
    return total, (coef * text_inverse).astype(BF16), (coef * image_inverse).astype(BF16)


def near(scalar_ref, i0, ia, ib, t0, t1, s0, t0x, t1x, s0x,
         images, texts, image_inverse, text_inverse, loss, by_text, by_image):
    for n, ref in enumerate((i0, ia, ib)):
        images[pl.ds(n * ROWS, ROWS), :] = ref[...]
    for n, ref in enumerate((t0, t1, s0, t0x, t1x, s0x)):
        texts[pl.ds(n * ROWS, ROWS), :] = ref[...]
    column = inverse_norm(images[...])
    image_inverse[...] = jnp.broadcast_to(column, image_inverse.shape)
    total = jnp.zeros((8, 128), F32)
    for tile in range(3):
        span = pl.ds(tile * TILE, TILE)
        block = texts[span, :]
        row = as_row(inverse_norm(block))
        text_inverse[:, span] = jnp.broadcast_to(row, (8, TILE))
        part, by_text[:, span], by_image[:, span] = terms(
            scalar_ref, dot_t(images[...], block), column, row, own=tile == 0)
        total = total + part
    loss[...] = total


def near_sums(by_text, by_image, images, texts, ht1, hs0, htx, hi):
    update = t_dot(by_image[:, ROWS:3 * ROWS], images[...])
    ht1[...] = update[:ROWS]
    hs0[...] = update[ROWS:]
    htx[...] = t_dot(by_image[:, 3 * ROWS:], images[...])
    hi[...] = dot(by_text[pl.ds(ROWS, 2 * ROWS), :], texts[...])


def own_sums(near_by_text, near_by_image, by_near_image, by_far_text, images, texts, i2, pair, own_text, own_image):
    own_text[...] = t_dot(near_by_image[:, :ROWS], images[...]) + t_dot(by_near_image[:, :ROWS], i2[...])
    own_image[...] = dot(near_by_text[pl.ds(0, ROWS), :], texts[...]) + dot(by_far_text[pl.ds(0, ROWS), :], pair[...])


def far(scalar_ref, i2, s1, sx, images, texts, image_inverse, text_inverse, loss_in,
        loss, by_near_text, by_near_image, by_far_text, by_far_image, four, pair):
    four[pl.ds(0, 3 * ROWS), :] = images[...]
    four[pl.ds(3 * ROWS, ROWS), :] = i2[...]
    pair[pl.ds(0, ROWS), :] = s1[...]
    pair[pl.ds(ROWS, ROWS), :] = sx[...]
    column = inverse_norm(i2[...])
    total, by_text, by_image = terms(scalar_ref, dot_t(i2[...], texts[...]), column, text_inverse[0:1, :])
    by_near_text[...] = by_text
    by_near_image[...] = by_image
    columns = jnp.concatenate([image_inverse[:, 0:1], column], axis=0)
    part, by_text, by_image = terms(
        scalar_ref, dot_t(four[...], pair[...]), columns, as_row(inverse_norm(pair[...])))
    by_far_text[...] = by_text
    by_far_image[...] = by_image
    loss[...] = loss_in[...] + total + part


def sums(core_ref, by_near_text, by_near_image, by_far_text, by_far_image, i2, four, pair, texts,
         ht1, hs0, htx, hi, blocks):
    second = core_ref[0]

    def put(on_first, on_second, value):
        at = pl.multiple_of((on_first + (on_second - on_first) * second) * ROWS, ROWS)
        blocks[pl.ds(at, ROWS), :] = value

    for n, old in ((1, ht1), (2, hs0)):
        value = old[...] + t_dot(by_near_image[:, n * ROWS:(n + 1) * ROWS], i2[...])
        put(7 + 2 * (n - 1), 1 + 2 * (n - 1) + 1, value)
    for n in range(3):
        value = htx[pl.ds(n * ROWS, ROWS), :] + t_dot(
            by_near_image[:, (n + 3) * ROWS:(n + 4) * ROWS], i2[...])
        if n == 0:
            blocks[pl.ds(0, ROWS), :] = value
        else:
            put(7 + 2 * (n - 1) + 1, 1 + 2 * (n - 1), value)
    value = t_dot(by_far_image[...], four[...])
    put(11, 6, value[:ROWS])
    put(12, 5, value[ROWS:])
    for n in range(3):
        put(2 + 2 * n, 7 + 2 * n, jnp.zeros_like(i2, dtype=F32))
    rest = dot(by_far_text[pl.ds(ROWS, 3 * ROWS), :], pair[...])
    for n in (1, 2):
        put(2 * n - 1, 6 + 2 * n, hi[pl.ds((n - 1) * ROWS, ROWS), :] + rest[(n - 1) * ROWS:n * ROWS])
    put(5, 12, dot(by_near_text[...], texts[...]) + rest[2 * ROWS:])


def everyone(loss, out):
    out[...] = jnp.broadcast_to(jnp.sum(loss[...], axis=0, keepdims=True), out.shape)


def finish(scalar_ref, image, text, image_hat, text_hat, parts, image_grad, text_grad, loss):
    for raw, hat_ref, out in ((image, image_hat, image_grad), (text, text_hat, text_grad)):
        inverse = inverse_norm(raw[...])
        unit = raw[...].astype(F32) * inverse
        hat = scalar_ref[0] * hat_ref[...]
        out[...] = (hat - unit * jnp.sum(unit * hat, axis=1, keepdims=True)) * inverse
    loss[0] = jnp.sum(parts[...]) / (ROWS * 256 * STEPS * ROWS * 16)


def inner(group, side, y):
    return group, 1 - side, y


def outer(group, side, y):
    return (group + 1) % 16, 1 - side, y


def outer_back(group, side, y):
    return (group + 15) % 16, 1 - side, y


def far_back(group, side, y):
    return (group + 15) % 16, side, y


def up(group, side, y):
    return group, side, (y + 1) % 4


def down(group, side, y):
    return group, side, (y + 3) % 4


def across(group, side, y):
    return group, side, (y + 2) % 4


def move(block, first, second=None):
    route = []
    for chip in range(128):
        place = (chip // 8, chip // 4 % 2, chip % 4)
        for core, to in enumerate((first, second or first)):
            group, side, y = to(*place)
            route.append((chip * 2 + core, (group * 8 + side * 4 + y) * 2 + core))
    return lax.ppermute(block, AXES, route)


def swap_cores(block):
    return lax.ppermute(block, "c", [(0, 1), (1, 0)])


def narrow(block):
    return (block * 16.0).astype(jnp.float16)


def widen(block):
    return block.astype(F32) * (1.0 / 16.0)


def together(*arrays):
    return lax.optimization_barrier(arrays)


def body(image_embed, text_embed, log_scale, logit_bias):
    width = image_embed.shape[1]
    scalars = jnp.stack([jnp.exp(log_scale[0]), logit_bias[0]])
    core = jnp.reshape(lax.axis_index("c"), (1,))
    first = lax.axis_index("c") == 0
    i0, t0 = image_embed, text_embed
    block = ((ROWS, width), F32)

    t1, s0 = move(t0, inner), move(t0, outer)
    ia, ib, t0x = move(i0, up), move(i0, down), swap_cores(t0)
    t1, s0 = together(t1, s0)
    s1 = move(jnp.where(first, t1, s0), outer, inner)
    ia, ib, t0x, t1, s0 = together(ia, ib, t0x, t1, s0)
    i2 = move(jnp.where(first, ia, ib), up, down)
    s0x, t1x = swap_cores(s0), swap_cores(t1)
    pairs = ((3 * ROWS, 6 * ROWS), BF16)
    images, texts, image_inverse, text_inverse, loss, near_by_text, near_by_image = call(
        near,
        (((3 * ROWS, width), BF16), ((6 * ROWS, width), BF16), ((3 * ROWS, 128), F32), ((8, 6 * ROWS), F32),
         ((8, 128), F32), pairs, pairs),
        8.0, 20, scalars, i0, ia, ib, t0, t1, s0, t0x, t1x, s0x)
    s1, loss = together(s1, loss)
    sx = swap_cores(s1)
    ht1, hs0, htx, hi = call(
        near_sums, (block, block, ((3 * ROWS, width), F32), ((2 * ROWS, width), F32)), 4.0, 20,
        near_by_text, near_by_image, images, texts)
    loss, by_near_text, by_near_image, by_far_text, by_far_image, four, pair = call(
        far,
        (((8, 128), F32), ((ROWS, 6 * ROWS), BF16), ((ROWS, 6 * ROWS), BF16), ((4 * ROWS, 2 * ROWS), BF16),
         ((4 * ROWS, 2 * ROWS), BF16), ((4 * ROWS, width), BF16), ((2 * ROWS, width), BF16)),
        2.0, 16, scalars, i2, s1, sx, images, texts, image_inverse, text_inverse, loss)
    loss_y = lax.ppermute(loss, "y", [(i, i ^ 1) for i in range(4)])
    blocks, = call(
        sums, (((13 * ROWS, width), F32),), 4.0, 28, core,
        by_near_text, by_near_image, by_far_text, by_far_image, i2, four, pair, texts, ht1, hs0, htx, hi)
    loss = loss + loss_y
    blocks, loss = together(blocks, loss)
    message = narrow(blocks[:7 * ROWS])
    other = swap_cores(message)
    loss = loss + move(loss, inner)
    own_text, own_image = call(
        own_sums, (block, block), 2.0, 20,
        near_by_text, near_by_image, by_near_image, by_far_text, images, texts, i2, pair)
    other, loss, own_text, own_image = together(other, loss, own_text, own_image)
    loss = loss + lax.ppermute(loss, "y", [(i, i ^ 2) for i in range(4)])
    own_text = own_text + widen(other[:ROWS])
    outs = [
        narrow(blocks[n * ROWS:(n + 2) * ROWS] + widen(other[(n - 6) * ROWS:(n - 4) * ROWS])) for n in (7, 9, 11)]
    back_far = move(outs[2], far_back, across)
    back_outer = move(outs[1], outer_back, up)
    back = (back_far, back_outer, move(outs[0], inner, down))
    loss, = call(everyone, (((32, 128), F32),), 20.0, 4, loss)
    loss = lax.all_to_all(loss, ("z", "xh", "c"), 0, 0, tiled=True)
    *back, loss = together(*back, loss)
    back = sum(widen(part) for part in back)
    stay = jnp.where(first, back[:ROWS], back[ROWS:])
    swapped = widen(swap_cores(narrow(jnp.where(first, back[ROWS:], back[:ROWS]))))
    text_hat = own_text + jnp.where(first, stay, swapped)
    image_hat = own_image + jnp.where(first, swapped, stay)
    image_grad, text_grad, loss = call(
        finish, (block, block, ((1,), F32)), 20.0, 12, scalars, image_embed, text_embed, image_hat, text_hat, loss)
    return loss, image_grad, text_grad


def solution(mesh):
    grid = Mesh(mesh.devices.reshape(SHAPE), AXES)
    rows = P(AXES, None)
    return jax.shard_map(
        body, mesh=grid, in_specs=(rows, rows, P(), P()), out_specs=(P(), rows, rows), check_vma=False)
```

```python
import jax
import jax.numpy as jnp
from jax import lax
from jax.experimental import pallas as pl
from jax.experimental.pallas import tpu as pltpu
from jax.sharding import Mesh, PartitionSpec as P

STEPS = 2
ROWS = 128
TILE = 256
AXES = ("z", "xh", "xl", "y", "c")
SHAPE = (8, 2, 2, 4, 2)
VMEM = pl.BlockSpec(memory_space=pltpu.VMEM)
SMEM = pl.BlockSpec(memory_space=pltpu.SMEM)
F32 = jnp.float32
BF16 = jnp.bfloat16


def call(kernel, outs, cost, limit, *args, scratch=()):
    shapes = tuple(jax.ShapeDtypeStruct(shape, dtype) for shape, dtype in outs)
    return pl.pallas_call(
        kernel,
        out_shape=shapes,
        in_specs=[SMEM if a.ndim == 1 else VMEM for a in args],
        out_specs=tuple(SMEM if len(s.shape) == 1 else VMEM for s in shapes),
        scratch_shapes=list(scratch),
        compiler_params=pltpu.CompilerParams(vmem_limit_bytes=limit * 2**20),
        cost_estimate=pl.CostEstimate(flops=int(cost * 1.0e9), bytes_accessed=int(cost * 3.0e6), transcendentals=0),
        name=kernel.__name__,
    )(*args)


def inverse_norm(rows):
    values = rows.astype(F32)
    return 1.0 / jnp.sqrt(jnp.sum(values * values, axis=1, keepdims=True) + 1e-06)


def as_row(column):
    eye = lax.broadcasted_iota(jnp.int32, (ROWS, ROWS), 0) == lax.broadcasted_iota(jnp.int32, (ROWS, ROWS), 1)
    parts = [
        jnp.sum(jnp.where(eye, column[n:n + ROWS], 0.0), axis=0, keepdims=True)
        for n in range(0, column.shape[0], ROWS)]
    return jnp.concatenate(parts, axis=1) if len(parts) > 1 else parts[0]


def dot_t(a, b):
    return lax.dot_general(a, b, (((1,), (1,)), ((), ())), preferred_element_type=F32)


def t_dot(a, b):
    return lax.dot_general(a, b, (((0,), (0,)), ((), ())), preferred_element_type=F32)


def dot(a, b):
    return jnp.dot(a, b, preferred_element_type=F32)


def terms(scalar_ref, products, image_inverse, text_inverse, own=False):
    z = products * (scalar_ref[0] * image_inverse) * text_inverse + scalar_ref[1]
    if own:
        row = lax.broadcasted_iota(jnp.int32, z.shape, 0)
        positive = (row == lax.broadcasted_iota(jnp.int32, z.shape, 1)) & (row < ROWS)
        z = jnp.where(positive, -z, z)
    small = jnp.exp(-jnp.abs(z))
    term = jnp.maximum(z, 0.0) + jnp.log1p(small)
    coef = jnp.where(z >= 0.0, 1.0, small) / (1.0 + small)
    if own:
        coef = jnp.where(positive, -coef, coef)
    total = sum(
        jnp.sum(term[:, n:n + 128].reshape(-1, 8, 128), axis=0) for n in range(0, z.shape[1], 128))
    return total, (coef * text_inverse).astype(BF16), (coef * image_inverse).astype(BF16)


def near(scalar_ref, i0, ia, ib, t0, t1, s0, t0x, t1x, s0x,
         images, texts, image_inverse, text_inverse, loss, by_text, by_image):
    for n, ref in enumerate((i0, ia, ib)):
        images[pl.ds(n * ROWS, ROWS), :] = ref[...]
    for n, ref in enumerate((t0, t1, s0, t0x, t1x, s0x)):
        texts[pl.ds(n * ROWS, ROWS), :] = ref[...]
    column = inverse_norm(images[...])
    image_inverse[...] = jnp.broadcast_to(column, image_inverse.shape)
    total = jnp.zeros((8, 128), F32)
    for tile in range(3):
        span = pl.ds(tile * TILE, TILE)
        block = texts[span, :]
        row = as_row(inverse_norm(block))
        text_inverse[:, span] = jnp.broadcast_to(row, (8, TILE))
        part, by_text[:, span], by_image[:, span] = terms(
            scalar_ref, dot_t(images[...], block), column, row, own=tile == 0)
        total = total + part
    loss[...] = total


def near_sums(by_text, by_image, images, texts, ht1, hs0, htx, hi):
    update = t_dot(by_image[:, ROWS:3 * ROWS], images[...])
    ht1[...] = update[:ROWS]
    hs0[...] = update[ROWS:]
    htx[...] = t_dot(by_image[:, 3 * ROWS:], images[...])
    hi[...] = dot(by_text[pl.ds(ROWS, 2 * ROWS), :], texts[...])


def own_sums(near_by_text, near_by_image, by_near_image, by_far_text, images, texts, i2, pair, own_text, own_image):
    own_text[...] = t_dot(near_by_image[:, :ROWS], images[...]) + t_dot(by_near_image[:, :ROWS], i2[...])
    own_image[...] = dot(near_by_text[pl.ds(0, ROWS), :], texts[...]) + dot(by_far_text[pl.ds(0, ROWS), :], pair[...])


def far(scalar_ref, i2, s1, sx, images, texts, image_inverse, text_inverse, loss_in,
        loss, by_near_text, by_near_image, by_far_text, by_far_image, four, pair):
    four[pl.ds(0, 3 * ROWS), :] = images[...]
    four[pl.ds(3 * ROWS, ROWS), :] = i2[...]
    pair[pl.ds(0, ROWS), :] = s1[...]
    pair[pl.ds(ROWS, ROWS), :] = sx[...]
    column = inverse_norm(i2[...])
    total, by_text, by_image = terms(scalar_ref, dot_t(i2[...], texts[...]), column, text_inverse[0:1, :])
    by_near_text[...] = by_text
    by_near_image[...] = by_image
    columns = jnp.concatenate([image_inverse[:, 0:1], column], axis=0)
    part, by_text, by_image = terms(
        scalar_ref, dot_t(four[...], pair[...]), columns, as_row(inverse_norm(pair[...])))
    by_far_text[...] = by_text
    by_far_image[...] = by_image
    loss[...] = loss_in[...] + total + part


def sums(core_ref, by_near_text, by_near_image, by_far_text, by_far_image, i2, four, pair, texts,
         ht1, hs0, htx, hi, blocks):
    second = core_ref[0]

    def put(on_first, on_second, value):
        at = pl.multiple_of((on_first + (on_second - on_first) * second) * ROWS, ROWS)
        blocks[pl.ds(at, ROWS), :] = value

    for n, old in ((1, ht1), (2, hs0)):
        value = old[...] + t_dot(by_near_image[:, n * ROWS:(n + 1) * ROWS], i2[...])
        put(7 + 2 * (n - 1), 1 + 2 * (n - 1) + 1, value)
    for n in range(3):
        value = htx[pl.ds(n * ROWS, ROWS), :] + t_dot(
            by_near_image[:, (n + 3) * ROWS:(n + 4) * ROWS], i2[...])
        if n == 0:
            blocks[pl.ds(0, ROWS), :] = value
        else:
            put(7 + 2 * (n - 1) + 1, 1 + 2 * (n - 1), value)
    value = t_dot(by_far_image[...], four[...])
    put(11, 6, value[:ROWS])
    put(12, 5, value[ROWS:])
    for n in range(3):
        put(2 + 2 * n, 7 + 2 * n, jnp.zeros_like(i2, dtype=F32))
    rest = dot(by_far_text[pl.ds(ROWS, 3 * ROWS), :], pair[...])
    for n in (1, 2):
        put(2 * n - 1, 6 + 2 * n, hi[pl.ds((n - 1) * ROWS, ROWS), :] + rest[(n - 1) * ROWS:n * ROWS])
    put(5, 12, dot(by_near_text[...], texts[...]) + rest[2 * ROWS:])


def everyone(loss, out):
    out[...] = jnp.broadcast_to(jnp.sum(loss[...], axis=0, keepdims=True), out.shape)


def finish(scalar_ref, image, text, image_inverse, image_hat, text_hat, parts, image_grad, text_grad, loss):
    for raw, hat_ref, out in ((image, image_hat, image_grad), (text, text_hat, text_grad)):
        inverse = image_inverse[pl.ds(0, ROWS), 0:1] if raw is image else inverse_norm(raw[...])
        unit = raw[...].astype(F32) * inverse
        hat = scalar_ref[0] * hat_ref[...]
        out[...] = (hat - unit * jnp.sum(unit * hat, axis=1, keepdims=True)) * inverse
    loss[0] = jnp.sum(parts[...]) / (ROWS * 256 * STEPS * ROWS * 16)


def inner(group, side, y):
    return group, 1 - side, y


def outer(group, side, y):
    return (group + 1) % 16, 1 - side, y


def outer_back(group, side, y):
    return (group + 15) % 16, 1 - side, y


def far_back(group, side, y):
    return (group + 15) % 16, side, y


def up(group, side, y):
    return group, side, (y + 1) % 4


def down(group, side, y):
    return group, side, (y + 3) % 4


def across(group, side, y):
    return group, side, (y + 2) % 4


def move(block, first, second=None):
    route = []
    for chip in range(128):
        place = (chip // 8, chip // 4 % 2, chip % 4)
        for core, to in enumerate((first, second or first)):
            group, side, y = to(*place)
            route.append((chip * 2 + core, (group * 8 + side * 4 + y) * 2 + core))
    return lax.ppermute(block, AXES, route)


def swap_cores(block):
    return lax.ppermute(block, "c", [(0, 1), (1, 0)])


def narrow(block):
    return (block * 16.0).astype(jnp.float16)


def widen(block):
    return block.astype(F32) * (1.0 / 16.0)


def together(*arrays):
    return lax.optimization_barrier(arrays)


def body(image_embed, text_embed, log_scale, logit_bias):
    width = image_embed.shape[1]
    scalars = jnp.stack([jnp.exp(log_scale[0]), logit_bias[0]])
    core = jnp.reshape(lax.axis_index("c"), (1,))
    first = lax.axis_index("c") == 0
    i0, t0 = image_embed, text_embed
    block = ((ROWS, width), F32)

    t1, s0 = move(t0, inner), move(t0, outer)
    ia, ib, t0x = move(i0, up), move(i0, down), swap_cores(t0)
    t1, s0 = together(t1, s0)
    s1 = move(jnp.where(first, t1, s0), outer, inner)
    ia, ib, t0x, t1, s0 = together(ia, ib, t0x, t1, s0)
    i2 = move(jnp.where(first, ia, ib), up, down)
    s0x, t1x = swap_cores(s0), swap_cores(t1)
    pairs = ((3 * ROWS, 6 * ROWS), BF16)
    images, texts, image_inverse, text_inverse, loss, near_by_text, near_by_image = call(
        near,
        (((3 * ROWS, width), BF16), ((6 * ROWS, width), BF16), ((3 * ROWS, 128), F32), ((8, 6 * ROWS), F32),
         ((8, 128), F32), pairs, pairs),
        8.0, 20, scalars, i0, ia, ib, t0, t1, s0, t0x, t1x, s0x)
    s1, loss = together(s1, loss)
    sx = swap_cores(s1)
    ht1, hs0, htx, hi = call(
        near_sums, (block, block, ((3 * ROWS, width), F32), ((2 * ROWS, width), F32)), 4.0, 20,
        near_by_text, near_by_image, images, texts)
    loss, by_near_text, by_near_image, by_far_text, by_far_image, four, pair = call(
        far,
        (((8, 128), F32), ((ROWS, 6 * ROWS), BF16), ((ROWS, 6 * ROWS), BF16), ((4 * ROWS, 2 * ROWS), BF16),
         ((4 * ROWS, 2 * ROWS), BF16), ((4 * ROWS, width), BF16), ((2 * ROWS, width), BF16)),
        2.0, 16, scalars, i2, s1, sx, images, texts, image_inverse, text_inverse, loss)
    loss_y = lax.ppermute(loss, "y", [(i, i ^ 1) for i in range(4)])
    blocks, = call(
        sums, (((13 * ROWS, width), F32),), 4.0, 28, core,
        by_near_text, by_near_image, by_far_text, by_far_image, i2, four, pair, texts, ht1, hs0, htx, hi)
    loss = loss + loss_y
    blocks, loss = together(blocks, loss)
    message = narrow(blocks[:7 * ROWS])
    other = swap_cores(message)
    loss = loss + move(loss, inner)
    own_text, own_image = call(
        own_sums, (block, block), 2.0, 20,
        near_by_text, near_by_image, by_near_image, by_far_text, images, texts, i2, pair)
    other, loss, own_text, own_image = together(other, loss, own_text, own_image)
    loss = loss + lax.ppermute(loss, "y", [(i, i ^ 2) for i in range(4)])
    own_text = own_text + widen(other[:ROWS])
    outs = [
        narrow(blocks[n * ROWS:(n + 2) * ROWS] + widen(other[(n - 6) * ROWS:(n - 4) * ROWS])) for n in (7, 9, 11)]
    back_far = move(outs[2], far_back, across)
    back_outer = move(outs[1], outer_back, up)
    back = (back_far, back_outer, move(outs[0], inner, down))
    loss, = call(everyone, (((32, 128), F32),), 20.0, 4, loss)
    loss = lax.all_to_all(loss, ("z", "xh", "c"), 0, 0, tiled=True)
    *back, loss = together(*back, loss)
    back = sum(widen(part) for part in back)
    stay = jnp.where(first, back[:ROWS], back[ROWS:])
    swapped = widen(swap_cores(narrow(jnp.where(first, back[ROWS:], back[:ROWS]))))
    text_hat = own_text + jnp.where(first, stay, swapped)
    image_hat = own_image + jnp.where(first, swapped, stay)
    image_grad, text_grad, loss = call(
        finish, (block, block, ((1,), F32)), 20.0, 12, scalars, image_embed, text_embed, image_inverse, image_hat, text_hat, loss)
    return loss, image_grad, text_grad


def solution(mesh):
    grid = Mesh(mesh.devices.reshape(SHAPE), AXES)
    rows = P(AXES, None)
    return jax.shard_map(
        body, mesh=grid, in_specs=(rows, rows, P(), P()), out_specs=(P(), rows, rows), check_vma=False)
```
